512 devices in a mesh: wide: 128 (over y, z, core), col: 4 (over x).
Axes of the slice: x: 4, y: 4, z: 16, core: 2. Of those that a mesh axis runs over, the one named last changes fastest.
Arguments:
- atom_feats: bfloat16 [65536, 128], P(('wide', 'col')), may hold values from -6 to 6
- atom_token: int32 [65536], P(('wide', 'col')), may hold values from 0 to 1023, as said below
- key_offset: int32 [2048], P(('wide', 'col')), may hold values from 0 to 32
- pair_in: bfloat16 [1024, 1024, 128], P('wide', 'col'), may hold values from -6 to 6
- w_qkv: bfloat16 [2, 128, 384], replicated, may hold values from -0.5 to 0.5
- w_out: bfloat16 [2, 128, 128], replicated, may hold values from -0.5 to 0.5
- w_up: bfloat16 [2, 128, 512], replicated, may hold values from -0.5 to 0.5
- w_down: bfloat16 [2, 256, 128], replicated, may hold values from -0.375 to 0.375
- w_tok: bfloat16 [128, 384], replicated, may hold values from -0.5 to 0.5
- w_row: bfloat16 [384, 128], replicated, may hold values from -0.3125 to 0.3125
- w_col: bfloat16 [384, 128], replicated, may hold values from -0.3125 to 0.3125
Outputs:
- atom_out: bfloat16 [65536, 128], P(('wide', 'col'))
- token_single: bfloat16 [1024, 384], P(('wide', 'col'))
- pair_out: bfloat16 [1024, 1024, 128], P('wide', 'col')
The draws below stay inside these ranges and needn't reach their ends.
Inputs may be any that keep to these rules, and one draw needn't show every extreme that they name: atom_token never falls, every token holds one atom or more, and for every atom l, floor(l / 64) - 1 <= atom_token[l] <= floor(l / 64).
All inputs are finite; a program needn't handle non-finite values.
Results may differ from the reference program's by a relative error of at most 0.012.
Values may be sent and summed in bfloat16 or wider, within the bound.
A program may use at most 64 MiB of HBM per device.

```python
import jax
import jax.numpy as jnp
from jax import lax

D = 128
HEADS = 4
HEAD = 32
FFH = 256
TOKC = 384
PAIRC = 128
QBLK = 32
KWIN = 128
LAYERS = 2
TOK_DEV = 8
PER_TOKEN = 64
ATOMS = 65536
TOKENS = 1024
BLOCKS = 2048
N_WIDE = 128


def draw_atom_token(key, part):
    key = jax.random.fold_in(key, 11)
    jitter = jax.random.randint(key, (TOKENS,), 0, PER_TOKEN, dtype=jnp.int32)
    jitter = jitter.at[0].set(0)
    atom_ids = jnp.arange(ATOMS, dtype=jnp.int32)
    nearest = atom_ids // PER_TOKEN
    return (nearest - (atom_ids % PER_TOKEN < jitter[nearest]).astype(jnp.int32)).astype(jnp.int32)


def draw_key_offset(key, part):
    key = jax.random.fold_in(key, 23)
    key_first, key_second, key_third = jax.random.split(key, 3)
    offsets = jax.random.randint(key_first, (BLOCKS,), 0, QBLK + 1, dtype=jnp.int32)
    first_pos = jax.random.randint(key_second, (), 0, BLOCKS, dtype=jnp.int32)
    second_pos = (first_pos + 1 + jax.random.randint(key_third, (), 0, BLOCKS - 1, dtype=jnp.int32)) % BLOCKS
    return offsets.at[first_pos].set(0).at[second_pos].set(QBLK)


def block_levels(own_key, shape, shards, low, high):
    loudness = 1.0
    for dim, blocks in shards:
        draws = jax.random.uniform(jax.random.fold_in(jax.random.fold_in(own_key, 6), dim), (blocks,), jnp.float32, low / len(shards), high / len(shards))
        loudness = loudness * jnp.repeat(jnp.exp(draws), shape[dim] // blocks).reshape((-1,) + (1,) * (len(shape) - 1 - dim))
    return loudness


def noise(key, extent, scale, limit, cuts=(), held_as=jnp.bfloat16):
    result = jax.random.normal(key, extent, jnp.float32) * scale
    if len(cuts) > 0:
        result = block_levels(key, extent, cuts, -0.22, 0.18) * result
    return jnp.clip(result, min=-limit, max=limit).astype(held_as)


def setup_inputs(seed: int = 0) -> dict:
    key_of = jax.random.split(jax.random.key(seed), 12)
    return {
        "atom_feats": noise(key_of[0], (ATOMS, D), 1.0, 6.0, ((0, 512),)),
        "atom_token": draw_atom_token(jax.random.fold_in(key_of[11], 71), 0),
        "key_offset": draw_key_offset(jax.random.fold_in(key_of[11], 71), 0),
        "pair_in": noise(key_of[3], (TOKENS, TOKENS, PAIRC), 1.0, 6.0, ((0, 128), (1, 4))),
        "w_qkv": noise(key_of[4], (LAYERS, D, 3 * D), D ** -0.5, 0.5),
        "w_out": noise(key_of[5], (LAYERS, D, D), D ** -0.5, 0.5),
        "w_up": noise(key_of[6], (LAYERS, D, 2 * FFH), D ** -0.5, 0.5),
        "w_down": noise(key_of[7], (LAYERS, FFH, D), FFH ** -0.5, 0.375),
        "w_tok": noise(key_of[8], (D, TOKC), D ** -0.5, 0.5),
        "w_row": noise(key_of[9], (TOKC, PAIRC), TOKC ** -0.5, 0.3125),
        "w_col": noise(key_of[10], (TOKC, PAIRC), TOKC ** -0.5, 0.3125),
    }


def normalize(values):
    row_mean = lax.optimization_barrier(jnp.mean(values, axis=-1, keepdims=True))
    centred = values - row_mean
    return centred * lax.rsqrt(lax.optimization_barrier(jnp.mean(centred * centred, axis=-1, keepdims=True)) + 1e-05)

def windows(queries, key_rows, value_rows, win_starts, key_valid):

    def take_window(start):
        return (lax.dynamic_slice_in_dim(key_rows, start, KWIN, 0), lax.dynamic_slice_in_dim(value_rows, start, KWIN, 0))
    key_win, value_win = jax.vmap(take_window)(win_starts)
    block_count = win_starts.shape[0]
    query_four = queries.reshape(block_count, QBLK, HEADS, HEAD).astype(jnp.float32)
    key_four = key_win.reshape(block_count, KWIN, HEADS, HEAD).astype(jnp.float32)
    value_four = value_win.reshape(block_count, KWIN, HEADS, HEAD).astype(jnp.float32)
    scores = jnp.einsum('bqhd,bkhd->bhqk', query_four, key_four) * (1.0 / HEAD ** 0.5)
    weights = jnp.exp(scores) * key_valid[:, None, None, :]
    weights = (weights / lax.optimization_barrier(jnp.sum(weights, axis=-1, keepdims=True))).astype(jnp.bfloat16)
    attended = jnp.einsum('bhqk,bkhd->bqhd', weights.astype(jnp.float32), value_four)
    return attended.reshape(block_count * QBLK, HEADS * HEAD).astype(jnp.bfloat16)

def reference(atom_feats, atom_token, key_offset, pair_in, w_qkv, w_out, w_up, w_down, w_tok, w_row, w_col):
    hidden_state = atom_feats.astype(jnp.float32)
    rim_width = KWIN - 2 * QBLK
    block_ids = jnp.arange(BLOCKS, dtype=jnp.int32)
    win_starts = (block_ids * QBLK + key_offset).astype(jnp.int32)
    key_pos = (win_starts - rim_width)[:, None] + jnp.arange(KWIN, dtype=jnp.int32)[None, :]
    key_valid = ((key_pos >= 0) & (key_pos < ATOMS)).astype(jnp.float32)
    for layer_idx in range(LAYERS):
        normed = normalize(hidden_state).astype(jnp.bfloat16)
        queries = jnp.dot(normed, w_qkv[layer_idx, :, :D], preferred_element_type=jnp.float32).astype(jnp.bfloat16)
        key_vals = jnp.dot(normed, w_qkv[layer_idx, :, D:], preferred_element_type=jnp.float32).astype(jnp.bfloat16)
        padded = jnp.pad(key_vals, ((rim_width, rim_width), (0, 0)))
        attended = windows(queries, padded[:, :D], padded[:, D:], win_starts, key_valid)
        hidden_state = hidden_state + jnp.dot(attended, w_out[layer_idx], preferred_element_type=jnp.float32)
        normed = normalize(hidden_state).astype(jnp.bfloat16)
        hidden = jnp.dot(normed, w_up[layer_idx], preferred_element_type=jnp.float32)
        gated_mid = (jax.nn.silu(hidden[:, :FFH]) * hidden[:, FFH:]).astype(jnp.bfloat16)
        hidden_state = hidden_state + jnp.dot(gated_mid, w_down[layer_idx], preferred_element_type=jnp.float32)
    atom_out = hidden_state.astype(jnp.bfloat16)
    tok_act = jax.nn.relu(jnp.dot(atom_out, w_tok, preferred_element_type=jnp.float32)).astype(jnp.bfloat16)
    tok_sums = jax.ops.segment_sum(tok_act.astype(jnp.float32), atom_token, num_segments=TOKENS)
    counts = jax.ops.segment_sum(jnp.ones((ATOMS,), jnp.float32), atom_token, num_segments=TOKENS)
    token_single = (tok_sums / counts[:, None]).astype(jnp.bfloat16)
    row_proj = jnp.dot(token_single, w_row, preferred_element_type=jnp.float32).astype(jnp.bfloat16)
    col_proj = jnp.dot(token_single, w_col, preferred_element_type=jnp.float32).astype(jnp.bfloat16)

    def add_rows(inputs):
        pair_tile, row_vecs = inputs
        summed = pair_tile.astype(jnp.float32) + row_vecs[:, None, :].astype(jnp.float32)
        return (summed + col_proj[None, :, :].astype(jnp.float32)).astype(jnp.bfloat16)
    pair_tiles = pair_in.reshape(N_WIDE, TOK_DEV, TOKENS, PAIRC)
    row_tiles = row_proj.reshape(N_WIDE, TOK_DEV, PAIRC)
    pair_out = lax.map(add_rows, (pair_tiles, row_tiles)).reshape(TOKENS, TOKENS, PAIRC)
    return (atom_out, token_single, pair_out)
```

```python
import functools

import jax
import jax.numpy as jnp
from jax import lax
from jax.experimental import pallas as pl
from jax.experimental.pallas import tpu as pltpu
from jax.sharding import PartitionSpec as P

D = 128
HEADS = 4
HEAD = 32
FFH = 256
TOKC = 384
QBLK = 32
KWIN = 128
RIM = 64
ROWS = 128
NY, NZ, NX = 4, 16, 4
SPREAD = 2
GROUP = NZ // SPREAD
STEPS = [d for d in range(-(GROUP // 2) + 1, GROUP // 2 + 1) if d != 0]
SCORE = 1.4426950408889634 / HEAD**0.5
NEG = -1e30
MESH = pl.DeviceIdType.MESH
f32, bf16 = jnp.float32, jnp.bfloat16


def device(y, z, core, x):
    return ((y * NZ + z) * 2 + core, x)


def along(step):
    at = lax.rem(lax.axis_index("wide") * NX + lax.axis_index("col") + step + 512, 512)
    return (at // NX, lax.rem(at, NX))


def dot(a, b):
    return jnp.dot(a, b, preferred_element_type=f32)


def norm(v):
    c = v - jnp.mean(v, axis=-1, keepdims=True)
    return (c * lax.rsqrt(jnp.mean(c * c, axis=-1, keepdims=True) + 1e-5)).astype(bf16)


def window_bias(offsets, first_block, query_row, n_query, n_key, base, n_atoms):
    parts = []
    for k in range(n_query // QBLK):
        off = offsets[first_block + k] + float(k * QBLK)
        key = lax.broadcasted_iota(jnp.int32, (QBLK, n_key), 1)
        rel = key.astype(f32) - off
        seen = (rel >= 0.0) & (rel < float(KWIN))
        pos = key + (base + query_row - RIM)
        here = (pos >= 0) & (pos < n_atoms)
        q_at = base + query_row + k * QBLK
        outside = (q_at < 0) | (q_at >= n_atoms)
        seen = seen & (here | outside)
        parts.append(jnp.where(seen, 0.0, NEG))
    return jnp.concatenate(parts, axis=0)


def attend(q, k, v, bias):
    n = q.shape[0]
    lane = lax.broadcasted_iota(jnp.int32, (n, D), 1) // HEAD
    stacked = jnp.concatenate(
        [jnp.where(lane == h, q, jnp.zeros_like(q)) for h in range(HEADS)], axis=0
    )
    scores = lax.dot_general(stacked, k, (((1,), (1,)), ((), ())), preferred_element_type=f32)
    weights = []
    for h in range(HEADS):
        e = jnp.exp2(scores[h * n : (h + 1) * n] * SCORE + bias)
        weights.append((e / jnp.sum(e, axis=-1, keepdims=True)).astype(bf16))
    out = dot(jnp.concatenate(weights, axis=0), v)
    total = jnp.zeros((n, D), f32)
    for h in range(HEADS):
        total = jnp.where(lane == h, out[h * n : (h + 1) * n], total)
    return total.astype(bf16)


def block(state, groups, biases, wq, wo, wu, wd):
    proj = dot(norm(state), wq).astype(bf16)
    kept = []
    for (row, n), bias in zip(groups, biases):
        lo, hi = row - RIM, row + n + RIM
        kept.append(attend(proj[row : row + n, :D], proj[lo:hi, D : 2 * D], proj[lo:hi, 2 * D :], bias))
    first = groups[0][0]
    last = groups[-1][0] + groups[-1][1]
    state = state[first:last] + dot(jnp.concatenate(kept, axis=0), wo)
    hidden = dot(norm(state), wu)
    gate, up = hidden[:, :FFH], hidden[:, FFH:]
    gated = (0.5 * gate * (1.0 + jnp.tanh(0.5 * gate)) * up).astype(bf16)
    return state + dot(gated, wd)


def kernel(
    n_atoms,
    feats, tok, koff, w_qkv, w_out, w_up, w_down, w_tok, w_row, w_col,
    atom_out, single, rows_out, cols_out,
    halo, far, wq, wo, wu, wd, wt, wp, mine, rowbuf, col_a, asm, gbuf,
    wsem, hsend, hrecv, rsend, rrecv, asend, arecv, bsend, brecv,
):
    wide, x = lax.axis_index("wide"), lax.axis_index("col")
    core = lax.rem(wide, 2)
    z = lax.rem(wide // 2, NZ)
    y = wide // (2 * NZ)
    me = wide * NX + x
    residue = lax.rem(z, GROUP)
    slot_a = (z // GROUP) * 8 + core * 4 + x
    home = x == y

    own = pltpu.make_async_copy(feats, halo.at[1, pl.ds(0, ROWS)], wsem.at[0])
    own.start()
    loads = []
    for n, (src, dst) in enumerate(
        [(w_qkv, wq), (w_out, wo), (w_up, wu), (w_down, wd), (w_tok, wt),
         (w_row, wp.at[:, pl.ds(0, D)]), (w_col, wp.at[:, pl.ds(D, D)])]
    ):
        loads.append(pltpu.make_async_copy(src, dst, wsem.at[n + 1]))
        loads[-1].start()

    barrier = pltpu.get_barrier_semaphore()

    def greet(dev):
        pl.semaphore_signal(barrier, inc=1, device_id=dev, device_id_type=MESH)

    for step in (-1, 1, 2):
        greet(along(step))
    for d in range(1, NX):
        greet((wide, lax.rem(x + d, NX)))
    for k in range(SPREAD):
        for c in range(2):
            for xs in range(NX):
                self_case = (home & (core == c) & (xs == x)) if k == 0 else None
                dev = device(x, lax.rem(z + k * GROUP, NZ), c, xs)
                if self_case is None:
                    greet(dev)
                else:
                    pl.when(jnp.logical_not(self_case))(functools.partial(greet, dev))
    for d in STEPS:
        greet(device(y, lax.rem(z - d + NZ, NZ), core, x))

    lanes = lax.broadcasted_iota(jnp.int32, (16, D), 0)
    tok_rel = (tok[...] - 2 * me).astype(f32)
    off4 = koff[...].astype(f32)
    offs = jnp.concatenate([off4] + [jnp.zeros((1, 4), f32)] * (D // 4 - 1), axis=1)
    meta = jnp.where(lanes == 0, tok_rel, jnp.where(lanes == 1, offs, 0.0))
    halo[1, pl.ds(ROWS, 16)] = meta.astype(bf16)
    own.wait()
    pl.semaphore_wait(barrier, 3 + 3 + 8 * SPREAD + len(STEPS) - home.astype(jnp.int32))

    sends = [
        pltpu.make_async_remote_copy(halo.at[1], halo.at[0], hsend.at[0], hrecv.at[0], along(1), MESH),
        pltpu.make_async_remote_copy(halo.at[1], halo.at[2], hsend.at[1], hrecv.at[1], along(-1), MESH),
        pltpu.make_async_remote_copy(
            halo.at[1, pl.ds(0, RIM)], far, hsend.at[2], hrecv.at[2], along(-2), MESH
        ),
    ]
    for s in sends:
        s.start()
    for load in loads:
        load.wait()
    for s in sends:
        s.wait_recv()

    metas = [halo[s, pl.ds(ROWS, 16)].astype(f32) for s in range(3)]
    offsets = [m[1:2, b : b + 1] for m in metas for b in range(4)]
    base = me * ROWS - ROWS
    spans1 = [(64, 128), (192, 128), (320, 64)]
    bias1 = [
        window_bias(offsets, row // QBLK, row, n, n + 2 * RIM, base, n_atoms) for row, n in spans1
    ]
    spans2 = [(64, 128), (192, 64)]
    bias2 = [
        window_bias(offsets, row // QBLK + 2, row, n, n + 2 * RIM, base + RIM, n_atoms)
        for row, n in spans2
    ]
    state = jnp.concatenate(
        [halo[0, pl.ds(0, ROWS)], halo[1, pl.ds(0, ROWS)], halo[2, pl.ds(0, ROWS)], far[...]], axis=0
    ).astype(f32)
    state = block(state, spans1, bias1, wq[0], wo[0], wu[0], wd[0])
    state = block(state, spans2, bias2, wq[1], wo[1], wu[1], wd[1])
    atoms = state.astype(bf16)
    atom_out[...] = atoms[:ROWS]

    act = jnp.maximum(dot(atoms, wt[...]), 0.0).astype(bf16)
    rel = jnp.concatenate([metas[1][0:1, :], metas[2][0:1, :RIM] + 2.0], axis=1)
    match = jnp.where(
        lax.broadcasted_iota(jnp.int32, (16, ROWS + RIM), 0).astype(f32) == rel, 1.0, 0.0
    )
    counts = jnp.maximum(jnp.sum(match, axis=-1, keepdims=True), 1.0)
    means = (dot(match.astype(bf16), act) / counts).astype(bf16)
    single[...] = means[0:2]
    proj = dot(means, wp[...]).astype(bf16).astype(f32)
    mine[0] = proj[0:2, :D]
    mine[1] = proj[0:2, D:]
    rowbuf[pl.ds(x, 1)] = proj[0:2, :D].reshape(1, 2, D)

    for k in range(SPREAD):
        zd = lax.rem(z + k * GROUP, NZ)
        for yd in range(NY):
            for c in range(2):
                def send_a(zd=zd, yd=yd, c=c):
                    pltpu.make_async_remote_copy(
                        mine.at[1], col_a.at[slot_a], asend, arecv, device(yd, zd, c, y), MESH
                    ).start()
                if k == 0:
                    self_case = home & (core == c) & (y == yd)
                    pl.when(jnp.logical_not(self_case))(send_a)
                else:
                    send_a()
    own_a = pltpu.make_async_copy(mine.at[1], col_a.at[slot_a], arecv)
    pl.when(home)(own_a.start)
    for d in range(1, NX):
        pltpu.make_async_remote_copy(
            mine.at[0], rowbuf.at[x], rsend, rrecv, (wide, lax.rem(x + d, NX)), MESH
        ).start()
    pltpu.make_async_copy(col_a, col_a, arecv).wait()

    for s in range(8 * SPREAD):
        asm[pl.ds(2 * s, 2), :] = col_a[s]
    gbuf[pl.ds(residue, 1)] = asm[...].astype(bf16).reshape(1, 16 * SPREAD, D)

    for d in STEPS:
        pltpu.make_async_remote_copy(
            gbuf.at[residue], gbuf.at[residue], bsend, brecv,
            device(y, lax.rem(z + d + NZ, NZ), core, x), MESH,
        ).start()
    rest = gbuf.at[pl.ds(0, len(STEPS))]
    pltpu.make_async_copy(rowbuf.at[pl.ds(0, 3)], rowbuf.at[pl.ds(0, 3)], rrecv).wait()
    for s in range(NX):
        rows_out[pl.ds(2 * s, 2), :] = rowbuf[s]
    pltpu.make_async_copy(rest, rest, brecv).wait()
    for r in range(GROUP):
        for k in range(SPREAD):
            cols_out[pl.ds((k * GROUP + r) * 16, 16), :] = gbuf[r, pl.ds(16 * k, 16)]

    for s in sends:
        s.wait_send()
    pltpu.make_async_copy(rowbuf.at[pl.ds(0, 3)], rowbuf.at[pl.ds(0, 3)], rsend).wait()
    less = col_a.at[pl.ds(0, 8 * SPREAD - 1)]
    pl.when(home)(pltpu.make_async_copy(less, less, asend).wait)
    pl.when(jnp.logical_not(home))(pltpu.make_async_copy(col_a, col_a, asend).wait)
    pltpu.make_async_copy(rest, rest, bsend).wait()


def on_device(
    atom_feats, atom_token, key_offset, pair_in, w_qkv, w_out, w_up, w_down, w_tok, w_row, w_col
):
    vmem = pl.BlockSpec(memory_space=pltpu.VMEM)
    hbm = pl.BlockSpec(memory_space=pl.ANY)
    dma = pltpu.SemaphoreType.DMA
    atom_out, single, row_vecs, col_vecs = pl.pallas_call(
        functools.partial(kernel, 512 * ROWS),
        out_shape=[
            jax.ShapeDtypeStruct((ROWS, D), bf16),
            jax.ShapeDtypeStruct((2, TOKC), bf16),
            jax.ShapeDtypeStruct((8, D), f32),
            jax.ShapeDtypeStruct((256, D), bf16),
        ],
        in_specs=[hbm, vmem, vmem] + [hbm] * 7,
        out_specs=[vmem] * 4,
        scratch_shapes=[
            pltpu.VMEM((3, ROWS + 16, D), bf16),
            pltpu.VMEM((RIM, D), bf16),
            pltpu.VMEM((2, D, 3 * D), bf16),
            pltpu.VMEM((2, D, D), bf16),
            pltpu.VMEM((2, D, 2 * FFH), bf16),
            pltpu.VMEM((2, FFH, D), bf16),
            pltpu.VMEM((D, TOKC), bf16),
            pltpu.VMEM((TOKC, 2 * D), bf16),
            pltpu.VMEM((2, 2, D), f32),
            pltpu.VMEM((NX, 2, D), f32),
            pltpu.VMEM((8 * SPREAD, 2, D), f32),
            pltpu.VMEM((16 * SPREAD, D), f32),
            pltpu.VMEM((GROUP, 16 * SPREAD, D), bf16),
            dma((8,)), dma((3,)), dma((3,)), dma, dma, dma, dma, dma, dma,
        ],
        compiler_params=pltpu.CompilerParams(
            collective_id=1, has_side_effects=True, vmem_limit_bytes=32 * 1024 * 1024
        ),
        name="atoms_tokens",
    )(
        atom_feats, atom_token.reshape(1, ROWS), key_offset.reshape(1, 4),
        w_qkv, w_out, w_up, w_down, w_tok, w_row, w_col,
    )
    summed = pair_in.astype(f32) + row_vecs[:, None, :]
    pair_out = (summed + col_vecs[None, :, :].astype(f32)).astype(bf16)
    return (atom_out, single, pair_out)


def solution(mesh):
    return jax.shard_map(
        on_device,
        mesh=mesh,
        in_specs=(
            P(("wide", "col"), None),
            P(("wide", "col")),
            P(("wide", "col")),
            P("wide", "col", None),
            P(), P(), P(), P(), P(), P(), P(),
        ),
        out_specs=(P(("wide", "col"), None), P(("wide", "col"), None), P("wide", "col", None)),
        check_vma=False,
    )
```

```python
import functools

import jax
import jax.numpy as jnp
from jax import lax
from jax.experimental import pallas as pl
from jax.experimental.pallas import tpu as pltpu
from jax.sharding import PartitionSpec as P

D = 128
HEADS = 4
HEAD = 32
FFH = 256
TOKC = 384
QBLK = 32
KWIN = 128
RIM = 64
ROWS = 128
NY, NZ, NX = 4, 16, 4
NEAR = (4, -4, 3, -3, 2, -2, 1, -1)
SCORE = 1.4426950408889634 / HEAD**0.5
NEG = -1e30
MESH = pl.DeviceIdType.MESH
f32, bf16 = jnp.float32, jnp.bfloat16


def device(y, z, core, x):
    return ((y * NZ + z) * 2 + core, x)


def along(step):
    at = lax.rem(lax.axis_index("wide") * NX + lax.axis_index("col") + step + 512, 512)
    return (at // NX, lax.rem(at, NX))


def dot(a, b):
    return jnp.dot(a, b, preferred_element_type=f32)


def norm(v):
    c = v - jnp.mean(v, axis=-1, keepdims=True)
    return (c * lax.rsqrt(jnp.mean(c * c, axis=-1, keepdims=True) + 1e-5)).astype(bf16)


def window_bias(offset, block, base, n_key, n_atoms):
    first = base - RIM
    at = base + block * QBLK
    outside = (at < 0) | (at >= n_atoms)
    floor = jnp.where(outside, -KWIN * 8, -first).astype(f32)
    ceil = jnp.where(outside, KWIN * 8, n_atoms - first).astype(f32)
    low = jnp.maximum(offset + float(block * QBLK), floor)
    high = jnp.minimum(offset + float(block * QBLK + KWIN), ceil)
    key = lax.broadcasted_iota(jnp.int32, (1, n_key), 1).astype(f32)
    return jnp.where((key >= low) & (key < high), 0.0, NEG)


def rows_of(blocks, n_key):
    return jnp.concatenate([jnp.broadcast_to(b[:, :n_key], (QBLK, n_key)) for b in blocks], axis=0)


def attend(q, k, v, bias):
    n = q.shape[0]
    lane = lax.broadcasted_iota(jnp.int32, (n, D), 1) // HEAD
    stacked = jnp.concatenate(
        [jnp.where(lane == h, q, jnp.zeros_like(q)) for h in range(HEADS)], axis=0
    )
    scores = lax.dot_general(stacked, k, (((1,), (1,)), ((), ())), preferred_element_type=f32)
    weights = []
    for h in range(HEADS):
        e = jnp.exp2(scores[h * n : (h + 1) * n] * SCORE + bias)
        weights.append((e / jnp.sum(e, axis=-1, keepdims=True)).astype(bf16))
    out = dot(jnp.concatenate(weights, axis=0), v)
    total = jnp.zeros((n, D), f32)
    for h in range(HEADS):
        total = jnp.where(lane == h, out[h * n : (h + 1) * n], total)
    return total.astype(bf16)


def block(state, proj, spans, biases, wo, wu, wd):
    kept = []
    for (row, n), bias in zip(spans, biases):
        lo, hi = row - RIM, row + n + RIM
        kept.append(
            attend(proj[row : row + n, :D], proj[lo:hi, D : 2 * D], proj[lo:hi, 2 * D :], bias)
        )
    first = spans[0][0]
    last = spans[-1][0] + spans[-1][1]
    state = state[first:last] + dot(jnp.concatenate(kept, axis=0), wo)
    hidden = dot(norm(state), wu)
    gate, up = hidden[:, :FFH], hidden[:, FFH:]
    gated = (0.5 * gate * (1.0 + jnp.tanh(0.5 * gate)) * up).astype(bf16)
    return state + dot(gated, wd)


def project(rows, wq):
    return dot(norm(rows), wq).astype(bf16)


def tokens(atoms, match, counts, wt, wp):
    act = jnp.maximum(dot(atoms, wt), 0.0).astype(bf16)
    means = (dot(match, act) / counts).astype(bf16)
    return means, dot(means, wp).astype(bf16)


def matches(own_meta, right_meta):
    rel = jnp.concatenate([own_meta[0:1, :], right_meta[0:1, :RIM] + 2.0], axis=1)
    ids = lax.broadcasted_iota(jnp.int32, (16, ROWS + RIM), 0).astype(f32)
    match = jnp.where(ids == rel, 1.0, 0.0)
    return match.astype(bf16), jnp.maximum(jnp.sum(match, axis=-1, keepdims=True), 1.0)


def biases_of(metas, base, n_atoms):
    out = []
    for start, n, n_key in ((-RIM, RIM, 192), (0, ROWS, 256), (ROWS, ROWS, 256)):
        span = []
        for k in range(n // QBLK):
            at = (start + ROWS) // QBLK + k
            off = metas[at // 4][1:2, at % 4 : at % 4 + 1]
            span.append(window_bias(off, k, base + start, n_key, n_atoms))
        out.append(span)
    return out


SPANS1 = [(64, 64), (128, 128), (256, 128)]
SPANS2 = [(64, 128), (192, 64)]


def transform(pieces, own_proj, metas, base, n_atoms, wq, wo, wu, wd):
    left, own, right, far = pieces
    biases = biases_of(metas, base, n_atoms)
    rim = project(jnp.concatenate([left, right, far], axis=0), wq[0])
    proj = jnp.concatenate([rim[:ROWS], own_proj, rim[ROWS:]], axis=0)
    state = jnp.concatenate([left, own, right, far], axis=0)
    bias1 = [rows_of(biases[0], 192), rows_of(biases[1], 256), rows_of(biases[2], 256)]
    state = block(state, proj, SPANS1, bias1, wo[0], wu[0], wd[0])
    bias2 = [bias1[1], rows_of(biases[2][:2], 192)]
    proj = project(state, wq[1])
    return block(state, proj, SPANS2, bias2, wo[1], wu[1], wd[1])


def peers():
    every = [(dy, dz, dc) for dy in range(NY) for dz in range(-7, 9) for dc in range(2)]
    return sorted(every, key=lambda o: (-(min(o[0], NY - o[0]) + abs(o[1])), -o[2]))


def kernel(
    n_atoms,
    feats, tok, koff, w_qkv, w_out, w_up, w_down, w_tok, w_row, w_col,
    atom_out, single, rows_out, cols_out,
    halo, far, toks, offs, wq, wo, wu, wd, wt, wp, mine, rowbuf, colbuf,
    wsem, hsend, hrecv, rsend, rrecv, csend, crecv, around, beyond,
):
    wide, x = lax.axis_index("wide"), lax.axis_index("col")
    core = lax.rem(wide, 2)
    z = lax.rem(wide // 2, NZ)
    y = wide // (2 * NZ)
    me = wide * NX + x
    home = x == y

    loads = []
    for n, (src, dst) in enumerate(
        [(feats, halo.at[1, pl.ds(0, ROWS)]), (tok, toks), (koff, offs),
         (w_qkv, wq), (w_out, wo), (w_up, wu), (w_down, wd), (w_tok, wt),
         (w_row, wp.at[:, pl.ds(0, D)]), (w_col, wp.at[:, pl.ds(D, D)])]
    ):
        loads.append(pltpu.make_async_copy(src, dst, wsem.at[n]))
        loads[-1].start()

    def tell(sem, dev):
        pl.semaphore_signal(sem, inc=1, device_id=dev, device_id_type=MESH)

    def beside(d):
        return device(y, lax.rem(z + d + NZ, NZ), core, x)

    barrier = pltpu.get_barrier_semaphore()
    for step in (-1, 1, 2):
        tell(barrier, along(step))
    for dy in range(NY):
        for dx in range(NX):
            for dc in range(2):
                if dy or dx or dc:
                    tell(
                        barrier,
                        device(lax.rem(y + dy, NY), z, lax.rem(core + dc, 2), lax.rem(x + dx, NX)),
                    )
    for d in NEAR:
        tell(barrier, beside(d))

    for load in loads[:3]:
        load.wait()
    row = lax.broadcasted_iota(jnp.int32, (16, D), 0)
    tok_rel = (toks[...] - 2 * me).astype(f32)
    off4 = jnp.concatenate(
        [offs[...].astype(f32)] + [jnp.zeros((1, 4), f32)] * (D // 4 - 1), axis=1
    )
    meta = jnp.where(row == 0, tok_rel, jnp.where(row == 1, off4, 0.0))
    halo[1, pl.ds(ROWS, 16)] = meta.astype(bf16)
    pl.semaphore_wait(barrier, 3 + 31 + len(NEAR))

    sends = [
        pltpu.make_async_remote_copy(
            halo.at[1], halo.at[0], hsend.at[0], hrecv.at[0], along(1), MESH
        ),
        pltpu.make_async_remote_copy(
            halo.at[1], halo.at[2], hsend.at[1], hrecv.at[1], along(-1), MESH
        ),
        pltpu.make_async_remote_copy(
            halo.at[1, pl.ds(0, RIM)], far, hsend.at[2], hrecv.at[2], along(-2), MESH
        ),
    ]
    for s in sends:
        s.start()

    for d in NEAR:
        tell(around, beside(d))
    loads[3].wait()
    own = halo[1, pl.ds(0, ROWS)].astype(f32)
    own_proj = project(own, wq[0])
    for load in loads[4:]:
        load.wait()
    for s in sends:
        s.wait_recv()
    pl.semaphore_wait(around, len(NEAR))
    for d in (4, -4):
        tell(beyond, beside(d))

    metas = [halo[s, pl.ds(ROWS, 16)].astype(f32) for s in range(3)]
    pieces = [halo[0, pl.ds(0, ROWS)].astype(f32), own]
    pieces += [halo[2, pl.ds(0, ROWS)].astype(f32), far[...].astype(f32)]
    match, counts = matches(metas[1], metas[2])
    state = transform(pieces, own_proj, metas, me * ROWS, n_atoms, wq, wo, wu, wd)
    atoms = state.astype(bf16)
    means, proj = tokens(atoms, match, counts, wt[...], wp[...])
    mine[0] = proj[0:2, :D]
    mine[1] = proj[0:2, D:]
    pl.semaphore_wait(beyond, 2)

    def send_column(dy, dz, dc):
        to = device(
            lax.rem(y + dy, NY), lax.rem(z + dz + NZ, NZ), lax.rem(core + dc, 2), y
        )
        pltpu.make_async_remote_copy(
            mine.at[1], colbuf.at[wide % 32 * NX + x], csend, crecv, to, MESH
        ).start()

    for dy, dz, dc in peers()[:-1]:
        send_column(dy, dz, dc)
    pl.when(jnp.logical_not(home))(functools.partial(send_column, 0, 0, 0))
    pl.when(home)(
        pltpu.make_async_copy(mine.at[1], colbuf.at[wide % 32 * NX + x], crecv).start
    )
    for d in range(1, NX):
        pltpu.make_async_remote_copy(
            mine.at[0], rowbuf.at[x], rsend, rrecv, (wide, lax.rem(x + d, NX)), MESH
        ).start()
    rowbuf[pl.ds(x, 1)] = proj[0:2, :D].reshape(1, 2, D)
    atom_out[...] = atoms[:ROWS]
    single[...] = means[0:2]

    three = rowbuf.at[pl.ds(0, 3)]
    pltpu.make_async_copy(three, three, rrecv).wait()
    for s in range(NX):
        rows_out[pl.ds(2 * s, 2), :] = rowbuf[s].astype(f32)
    for s in sends:
        s.wait_send()
    pltpu.make_async_copy(three, three, rsend).wait()
    less = colbuf.at[pl.ds(0, 127)]
    pl.when(home)(pltpu.make_async_copy(less, less, csend).wait)
    pl.when(jnp.logical_not(home))(pltpu.make_async_copy(colbuf, colbuf, csend).wait)
    pltpu.make_async_copy(colbuf, colbuf, crecv).wait()
    for s in range(128):
        cols_out[pl.ds(2 * s, 2), :] = colbuf[s].astype(f32)


def finish(pair, rows, cols, atoms, means, pair_out, atom_out, single, sums, sem):
    copies = [
        pltpu.make_async_copy(atoms, atom_out, sem.at[0]),
        pltpu.make_async_copy(means, single, sem.at[1]),
    ]
    for copy in copies:
        copy.start()
    cols = cols[...]
    for r in range(8):
        sums[r] = ((pair[r].astype(f32) + rows[pl.ds(r, 1), :]) + cols).astype(bf16)
        copies.append(pltpu.make_async_copy(sums.at[r], pair_out.at[r], sem.at[r + 2]))
        copies[-1].start()
    for copy in copies:
        copy.wait()


def on_device(
    atom_feats, atom_token, key_offset, pair_in, w_qkv, w_out, w_up, w_down, w_tok, w_row, w_col
):
    vmem = pl.BlockSpec(memory_space=pltpu.VMEM)
    hbm = pl.BlockSpec(memory_space=pltpu.HBM)
    dma, flag = pltpu.SemaphoreType.DMA, pltpu.SemaphoreType.REGULAR
    atoms, means, row_vecs, col_vecs = pl.pallas_call(
        functools.partial(kernel, 512 * ROWS),
        out_shape=[
            jax.ShapeDtypeStruct((ROWS, D), bf16),
            jax.ShapeDtypeStruct((2, TOKC), bf16),
            jax.ShapeDtypeStruct((8, D), f32),
            jax.ShapeDtypeStruct((256, D), f32),
        ],
        in_specs=[hbm] * 10,
        out_specs=[vmem] * 4,
        scratch_shapes=[
            pltpu.VMEM((3, ROWS + 16, D), bf16),
            pltpu.VMEM((RIM, D), bf16),
            pltpu.VMEM((1, ROWS), jnp.int32),
            pltpu.VMEM((1, 4), jnp.int32),
            pltpu.VMEM((2, D, 3 * D), bf16),
            pltpu.VMEM((2, D, D), bf16),
            pltpu.VMEM((2, D, 2 * FFH), bf16),
            pltpu.VMEM((2, FFH, D), bf16),
            pltpu.VMEM((D, TOKC), bf16),
            pltpu.VMEM((TOKC, 2 * D), bf16),
            pltpu.VMEM((2, 2, D), bf16),
            pltpu.VMEM((NX, 2, D), bf16),
            pltpu.VMEM((128, 2, D), bf16),
            dma((10,)), dma((3,)), dma((3,)), dma, dma, dma, dma, flag, flag,
        ],
        compiler_params=pltpu.CompilerParams(
            collective_id=1, has_side_effects=True, vmem_limit_bytes=32 * 1024 * 1024
        ),
        name="atoms_tokens",
    )(
        *[
            pltpu.with_memory_space_constraint(a, pltpu.HBM)
            for a in (
                atom_feats, atom_token.reshape(1, ROWS), key_offset.reshape(1, 4),
                w_qkv, w_out, w_up, w_down, w_tok, w_row, w_col,
            )
        ]
    )
    pair_out, atom_out, single = pl.pallas_call(
        finish,
        out_shape=[
            jax.ShapeDtypeStruct(pair_in.shape, bf16),
            jax.ShapeDtypeStruct((ROWS, D), bf16),
            jax.ShapeDtypeStruct((2, TOKC), bf16),
        ],
        in_specs=[vmem] * 5,
        out_specs=[hbm] * 3,
        scratch_shapes=[pltpu.VMEM(pair_in.shape, bf16), dma((10,))],
        compiler_params=pltpu.CompilerParams(vmem_limit_bytes=16 * 1024 * 1024),
        name="pair_add",
    )(pair_in, row_vecs, col_vecs, atoms, means)
    return (atom_out, single, pair_out)


def solution(mesh):
    return jax.shard_map(
        on_device,
        mesh=mesh,
        in_specs=(
            P(("wide", "col"), None),
            P(("wide", "col")),
            P(("wide", "col")),
            P("wide", "col", None),
            P(), P(), P(), P(), P(), P(), P(),
        ),
        out_specs=(P(("wide", "col"), None), P(("wide", "col"), None), P("wide", "col", None)),
        check_vma=False,
    )
```

```python
import functools

import jax
import jax.numpy as jnp
from jax import lax
from jax.experimental import pallas as pl
from jax.experimental.pallas import tpu as pltpu
from jax.sharding import PartitionSpec as P

D = 128
HEADS = 4
HEAD = 32
FFH = 256
TOKC = 384
QBLK = 32
KWIN = 128
RIM = 64
ROWS = 128
NY, NZ, NX = 4, 16, 4
NEAR = (4, -4, 3, -3, 2, -2, 1, -1)
SCORE = 1.4426950408889634 / HEAD**0.5
NEG = -1e30
MESH = pl.DeviceIdType.MESH
f32, bf16 = jnp.float32, jnp.bfloat16


def device(y, z, core, x):
    return ((y * NZ + z) * 2 + core, x)


def along(step):
    at = lax.rem(lax.axis_index("wide") * NX + lax.axis_index("col") + step + 512, 512)
    return (at // NX, lax.rem(at, NX))


def dot(a, b):
    return jnp.dot(a, b, preferred_element_type=f32)


def norm(v):
    c = v - jnp.mean(v, axis=-1, keepdims=True)
    return (c * lax.rsqrt(jnp.mean(c * c, axis=-1, keepdims=True) + 1e-5)).astype(bf16)


def window_bias(offset, block, base, n_key, n_atoms):
    first = base - RIM
    at = base + block * QBLK
    outside = (at < 0) | (at >= n_atoms)
    floor = jnp.where(outside, -KWIN * 8, -first).astype(f32)
    ceil = jnp.where(outside, KWIN * 8, n_atoms - first).astype(f32)
    low = jnp.maximum(offset + float(block * QBLK), floor)
    high = jnp.minimum(offset + float(block * QBLK + KWIN), ceil)
    key = lax.broadcasted_iota(jnp.int32, (1, n_key), 1).astype(f32)
    return jnp.where((key >= low) & (key < high), 0.0, NEG)


def rows_of(blocks, n_key):
    return jnp.concatenate([jnp.broadcast_to(b[:, :n_key], (QBLK, n_key)) for b in blocks], axis=0)


def attend(q, k, v, bias):
    n = q.shape[0]
    lane = lax.broadcasted_iota(jnp.int32, (n, D), 1) // HEAD
    stacked = jnp.concatenate(
        [jnp.where(lane == h, q, jnp.zeros_like(q)) for h in range(HEADS)], axis=0
    )
    scores = lax.dot_general(stacked, k, (((1,), (1,)), ((), ())), preferred_element_type=f32)
    weights = []
    for h in range(HEADS):
        e = jnp.exp2(scores[h * n : (h + 1) * n] * SCORE + bias)
        weights.append((e / jnp.sum(e, axis=-1, keepdims=True)).astype(bf16))
    out = dot(jnp.concatenate(weights, axis=0), v)
    total = jnp.zeros((n, D), f32)
    for h in range(HEADS):
        total = jnp.where(lane == h, out[h * n : (h + 1) * n], total)
    return total.astype(bf16)


def block(state, proj, spans, biases, wo, wu, wd):
    kept = []
    for (row, n), bias in zip(spans, biases):
        lo, hi = row - RIM, row + n + RIM
        kept.append(
            attend(proj[row : row + n, :D], proj[lo:hi, D : 2 * D], proj[lo:hi, 2 * D :], bias)
        )
    first = spans[0][0]
    last = spans[-1][0] + spans[-1][1]
    state = state[first:last] + dot(jnp.concatenate(kept, axis=0), wo)
    hidden = dot(norm(state), wu)
    gate, up = hidden[:, :FFH], hidden[:, FFH:]
    gated = (0.5 * gate * (1.0 + jnp.tanh(0.5 * gate)) * up).astype(bf16)
    return state + dot(gated, wd)


def project(rows, wq):
    return dot(norm(rows), wq).astype(bf16)


def tokens(atoms, match, counts, wt, wp):
    act = jnp.maximum(dot(atoms, wt), 0.0).astype(bf16)
    means = (dot(match, act) / counts).astype(bf16)
    return means, dot(means, wp).astype(bf16)


def matches(own_meta, right_meta):
    rel = jnp.concatenate([own_meta[0:1, :], right_meta[0:1, :RIM] + 2.0], axis=1)
    ids = lax.broadcasted_iota(jnp.int32, (16, ROWS + RIM), 0).astype(f32)
    match = jnp.where(ids == rel, 1.0, 0.0)
    return match.astype(bf16), jnp.maximum(jnp.sum(match, axis=-1, keepdims=True), 1.0)


def biases_of(metas, base, n_atoms):
    out = []
    for start, n, n_key in ((-RIM, RIM, 192), (0, ROWS, 256), (ROWS, ROWS, 256)):
        span = []
        for k in range(n // QBLK):
            at = (start + ROWS) // QBLK + k
            off = metas[at // 4][1:2, at % 4 : at % 4 + 1]
            span.append(window_bias(off, k, base + start, n_key, n_atoms))
        out.append(span)
    return out


SPANS1 = [(64, 64), (128, 128), (256, 128)]
SPANS2 = [(64, 128), (192, 64)]


def tell(sem, dev):
    pl.semaphore_signal(sem, inc=1, device_id=dev, device_id_type=MESH)


def halo_kernel(
    feats, tok, koff, w_qkv, w_out, w_up, w_down, w_tok, w_row, w_col,
    atoms, metas, wq, wo, wu, wd, wt, wp,
    halo, far, toks, offs, wsem, hsend, hrecv,
):
    me = lax.axis_index("wide") * NX + lax.axis_index("col")
    barrier = pltpu.get_barrier_semaphore()
    for step in (-1, 1):
        tell(barrier, along(step))
    loads = []
    for n, (src, dst) in enumerate(
        [(feats, halo.at[1, pl.ds(0, ROWS)]), (tok, toks), (koff, offs),
         (w_qkv, wq), (w_out, wo), (w_up, wu), (w_down, wd), (w_tok, wt),
         (w_row, wp.at[:, pl.ds(0, D)]), (w_col, wp.at[:, pl.ds(D, D)])]
    ):
        loads.append(pltpu.make_async_copy(src, dst, wsem.at[n]))
        loads[-1].start()

    for load in loads[:3]:
        load.wait()
    row = lax.broadcasted_iota(jnp.int32, (16, D), 0)
    tok_rel = (toks[...] - 2 * me).astype(f32)
    off4 = jnp.concatenate(
        [offs[...].astype(f32)] + [jnp.zeros((1, 4), f32)] * (D // 4 - 1), axis=1
    )
    meta = jnp.where(row == 0, tok_rel, jnp.where(row == 1, off4, 0.0))
    halo[1, pl.ds(ROWS, 16)] = meta.astype(bf16)
    pl.semaphore_wait(barrier, 2)

    left = pltpu.make_async_remote_copy(
        halo.at[1], halo.at[2], hsend.at[1], hrecv.at[1], along(-1), MESH
    )
    right = pltpu.make_async_remote_copy(
        halo.at[1], halo.at[0], hsend.at[0], hrecv.at[0], along(1), MESH
    )
    left.start()
    right.start()
    left.wait_recv()
    pass_on = pltpu.make_async_remote_copy(
        halo.at[2, pl.ds(0, RIM)], far, hsend.at[2], hrecv.at[2], along(-1), MESH
    )
    pass_on.start()
    right.wait_recv()
    for s in range(3):
        atoms[pl.ds(s * ROWS, ROWS), :] = halo[s, pl.ds(0, ROWS)]
        metas[pl.ds(s * 16, 16), :] = halo[s, pl.ds(ROWS, 16)]
    for load in loads[3:]:
        load.wait()
    pass_on.wait_recv()
    atoms[pl.ds(3 * ROWS, RIM), :] = far[...]
    for s in (left, right, pass_on):
        s.wait_send()


def kernel(
    n_atoms,
    atoms_in, metas_in, wq, wo, wu, wd, wt, wp,
    atom_out, single, rows_out, cols_out,
    mine, rowbuf, colbuf,
    rsend, rrecv, csend, crecv, around, beyond,
):
    wide, x = lax.axis_index("wide"), lax.axis_index("col")
    core = lax.rem(wide, 2)
    z = lax.rem(wide // 2, NZ)
    y = wide // (2 * NZ)
    me = wide * NX + x
    home = x == y
    side = (z > NZ // 2).astype(jnp.int32)
    sign = 2 * side - 1
    edge = (z < 4) | (z >= NZ - 4)

    def beside(d):
        return device(y, lax.rem(z + d + NZ, NZ), core, x)

    barrier = pltpu.get_barrier_semaphore()
    for d in NEAR:
        tell(barrier, beside(d))
    for xs in range(NX):
        for c in range(2):
            pl.when(jnp.logical_not(home & (core == c) & (xs == x)))(
                functools.partial(tell, barrier, device(x, z, c, xs))
            )
    for d in range(1, NX):
        tell(barrier, (wide, lax.rem(x + d, NX)))

    atoms_f = atoms_in[...].astype(f32)
    metas = [metas_in[pl.ds(16 * s, 16), :].astype(f32) for s in range(3)]
    match, counts = matches(metas[1], metas[2])
    biases = biases_of(metas, me * ROWS, n_atoms)
    bias1 = [rows_of(biases[0], 192), rows_of(biases[1], 256), rows_of(biases[2], 256)]
    state = block(atoms_f, project(atoms_f, wq[0]), SPANS1, bias1, wo[0], wu[0], wd[0])

    pl.semaphore_wait(barrier, 8 + 3 + len(NEAR) - home.astype(jnp.int32))
    for d in NEAR:
        tell(around.at[0 if d > 0 else 1], beside(d))

    bias2 = [bias1[1], rows_of(biases[2][:2], 192)]
    state = block(state, project(state, wq[1]), SPANS2, bias2, wo[1], wu[1], wd[1])
    atoms = state.astype(bf16)
    means, proj = tokens(atoms, match, counts, wt[...], wp[...])
    mine[0] = proj[0:2, :D]
    mine[1] = proj[0:2, D:]

    def pass_on(which, direction):
        pl.semaphore_wait(around.at[which], 4)
        tell(beyond.at[which], beside(-4 * direction))

    slot = lax.rem(wide, 32) * NX + x

    def send_columns(zd):
        for dy in (2, 1, 3, 0):
            for dc in (1, 0):
                to = device(lax.rem(y + dy, NY), zd, lax.rem(core + dc, 2), y)
                pltpu.make_async_remote_copy(
                    mine.at[1], colbuf.at[slot], csend, crecv, to, MESH
                ).start()

    pass_on(side, sign)
    pl.when(edge)(functools.partial(pass_on, 1 - side, -sign))
    pl.semaphore_wait(beyond.at[side], 1)
    for d in range(8, 0, -1):
        send_columns(lax.rem(z + sign * d + NZ, NZ))
    for dy in (2, 1, 3, 0):
        for dc in (1, 0):
            to = device(lax.rem(y + dy, NY), z, lax.rem(core + dc, 2), y)
            copy = pltpu.make_async_remote_copy(
                mine.at[1], colbuf.at[slot], csend, crecv, to, MESH
            )
            if dy or dc:
                copy.start()
            else:
                pl.when(jnp.logical_not(home))(copy.start)
    pl.when(home)(pltpu.make_async_copy(mine.at[1], colbuf.at[slot], crecv).start)
    for d in range(1, NX):
        pltpu.make_async_remote_copy(
            mine.at[0], rowbuf.at[x], rsend, rrecv, (wide, lax.rem(x + d, NX)), MESH
        ).start()
    pl.when(jnp.logical_not(edge))(functools.partial(pass_on, 1 - side, -sign))
    pl.semaphore_wait(beyond.at[1 - side], 1)
    for d in range(7, 0, -1):
        send_columns(lax.rem(z - sign * d + NZ, NZ))

    rowbuf[pl.ds(x, 1)] = proj[0:2, :D].reshape(1, 2, D)
    atom_out[...] = atoms[:ROWS]
    single[...] = means[0:2]

    three = rowbuf.at[pl.ds(0, 3)]
    pltpu.make_async_copy(three, three, rrecv).wait()
    for s in range(NX):
        rows_out[pl.ds(2 * s, 2), :] = rowbuf[s].astype(f32)
    pltpu.make_async_copy(three, three, rsend).wait()
    less = colbuf.at[pl.ds(0, 127)]
    pl.when(home)(pltpu.make_async_copy(less, less, csend).wait)
    pl.when(jnp.logical_not(home))(pltpu.make_async_copy(colbuf, colbuf, csend).wait)
    pltpu.make_async_copy(colbuf, colbuf, crecv).wait()
    for s in range(128):
        cols_out[pl.ds(2 * s, 2), :] = colbuf[s].astype(f32)


def finish(pair, rows, cols, atoms, means, pair_out, atom_out, single, sums, sem):
    copies = [
        pltpu.make_async_copy(atoms, atom_out, sem.at[0]),
        pltpu.make_async_copy(means, single, sem.at[1]),
    ]
    for copy in copies:
        copy.start()
    cols = cols[...]
    for r in range(8):
        sums[r] = ((pair[r].astype(f32) + rows[pl.ds(r, 1), :]) + cols).astype(bf16)
        copies.append(pltpu.make_async_copy(sums.at[r], pair_out.at[r], sem.at[r + 2]))
        copies[-1].start()
    for copy in copies:
        copy.wait()


def on_device(
    atom_feats, atom_token, key_offset, pair_in, w_qkv, w_out, w_up, w_down, w_tok, w_row, w_col
):
    vmem = pl.BlockSpec(memory_space=pltpu.VMEM)
    hbm = pl.BlockSpec(memory_space=pltpu.HBM)
    dma = pltpu.SemaphoreType.DMA
    near = pl.pallas_call(
        halo_kernel,
        out_shape=[
            jax.ShapeDtypeStruct((3 * ROWS + RIM, D), bf16),
            jax.ShapeDtypeStruct((48, D), bf16),
            jax.ShapeDtypeStruct((2, D, 3 * D), bf16),
            jax.ShapeDtypeStruct((2, D, D), bf16),
            jax.ShapeDtypeStruct((2, D, 2 * FFH), bf16),
            jax.ShapeDtypeStruct((2, FFH, D), bf16),
            jax.ShapeDtypeStruct((D, TOKC), bf16),
            jax.ShapeDtypeStruct((TOKC, 2 * D), bf16),
        ],
        in_specs=[hbm] * 10,
        out_specs=[vmem] * 8,
        scratch_shapes=[
            pltpu.VMEM((3, ROWS + 16, D), bf16),
            pltpu.VMEM((RIM, D), bf16),
            pltpu.VMEM((1, ROWS), jnp.int32),
            pltpu.VMEM((1, 4), jnp.int32),
            dma((10,)), dma((3,)), dma((3,)),
        ],
        compiler_params=pltpu.CompilerParams(
            collective_id=1, has_side_effects=True, vmem_limit_bytes=16 * 1024 * 1024
        ),
        name="halo",
    )(
        *[
            pltpu.with_memory_space_constraint(a, pltpu.HBM)
            for a in (
                atom_feats, atom_token.reshape(1, ROWS), key_offset.reshape(1, 4),
                w_qkv, w_out, w_up, w_down, w_tok, w_row, w_col,
            )
        ]
    )
    atoms, means, row_vecs, col_vecs = pl.pallas_call(
        functools.partial(kernel, 512 * ROWS),
        out_shape=[
            jax.ShapeDtypeStruct((ROWS, D), bf16),
            jax.ShapeDtypeStruct((2, TOKC), bf16),
            jax.ShapeDtypeStruct((8, D), f32),
            jax.ShapeDtypeStruct((256, D), f32),
        ],
        in_specs=[vmem] * 8,
        out_specs=[vmem] * 4,
        scratch_shapes=[
            pltpu.VMEM((2, 2, D), bf16),
            pltpu.VMEM((NX, 2, D), bf16),
            pltpu.VMEM((128, 2, D), bf16),
            dma, dma, dma, dma, pltpu.SemaphoreType.REGULAR((2,)), pltpu.SemaphoreType.REGULAR((2,)),
        ],
        compiler_params=pltpu.CompilerParams(
            collective_id=2, has_side_effects=True, vmem_limit_bytes=32 * 1024 * 1024
        ),
        name="atoms_tokens",
    )(*near)
    pair_out, atom_out, single = pl.pallas_call(
        finish,
        out_shape=[
            jax.ShapeDtypeStruct(pair_in.shape, bf16),
            jax.ShapeDtypeStruct((ROWS, D), bf16),
            jax.ShapeDtypeStruct((2, TOKC), bf16),
        ],
        in_specs=[vmem] * 5,
        out_specs=[hbm] * 3,
        scratch_shapes=[pltpu.VMEM(pair_in.shape, bf16), dma((10,))],
        compiler_params=pltpu.CompilerParams(vmem_limit_bytes=16 * 1024 * 1024),
        name="pair_add",
    )(pair_in, row_vecs, col_vecs, atoms, means)
    return (atom_out, single, pair_out)


def solution(mesh):
    return jax.shard_map(
        on_device,
        mesh=mesh,
        in_specs=(
            P(("wide", "col"), None),
            P(("wide", "col")),
            P(("wide", "col")),
            P("wide", "col", None),
            P(), P(), P(), P(), P(), P(), P(),
        ),
        out_specs=(P(("wide", "col"), None), P(("wide", "col"), None), P("wide", "col", None)),
        check_vma=False,
    )
```

```python
import functools

import jax
import jax.numpy as jnp
from jax import lax
from jax.experimental import pallas as pl
from jax.experimental.pallas import tpu as pltpu
from jax.sharding import PartitionSpec as P

D = 128
HEADS = 4
HEAD = 32
FFH = 256
TOKC = 384
QBLK = 32
KWIN = 128
RIM = 64
ROWS = 128
NY, NZ, NX = 4, 16, 4
NEAR = (4, -4, 3, -3, 2, -2, 1, -1)
SCORE = 1.4426950408889634 / HEAD**0.5
NEG = -1e30
MESH = pl.DeviceIdType.MESH
f32, bf16 = jnp.float32, jnp.bfloat16


def device(y, z, core, x):
    return ((y * NZ + z) * 2 + core, x)


def along(step):
    at = lax.rem(lax.axis_index("wide") * NX + lax.axis_index("col") + step + 512, 512)
    return (at // NX, lax.rem(at, NX))


def dot(a, b):
    return jnp.dot(a, b, preferred_element_type=f32)


def norm(v):
    c = v - jnp.mean(v, axis=-1, keepdims=True)
    return (c * lax.rsqrt(jnp.mean(c * c, axis=-1, keepdims=True) + 1e-5)).astype(bf16)


def window_bias(offset, block, base, n_key, n_atoms):
    first = base - RIM
    at = base + block * QBLK
    outside = (at < 0) | (at >= n_atoms)
    floor = jnp.where(outside, -KWIN * 8, -first).astype(f32)
    ceil = jnp.where(outside, KWIN * 8, n_atoms - first).astype(f32)
    low = jnp.maximum(offset + float(block * QBLK), floor)
    high = jnp.minimum(offset + float(block * QBLK + KWIN), ceil)
    key = lax.broadcasted_iota(jnp.int32, (1, n_key), 1).astype(f32)
    return jnp.where((key >= low) & (key < high), 0.0, NEG)


def rows_of(blocks, n_key):
    return jnp.concatenate([jnp.broadcast_to(b[:, :n_key], (QBLK, n_key)) for b in blocks], axis=0)


def attend(q, k, v, bias):
    n = q.shape[0]
    lane = lax.broadcasted_iota(jnp.int32, (n, D), 1) // HEAD
    stacked = jnp.concatenate(
        [jnp.where(lane == h, q, jnp.zeros_like(q)) for h in range(HEADS)], axis=0
    )
    scores = lax.dot_general(stacked, k, (((1,), (1,)), ((), ())), preferred_element_type=f32)
    weights = []
    for h in range(HEADS):
        e = jnp.exp2(scores[h * n : (h + 1) * n] * SCORE + bias)
        weights.append((e / jnp.sum(e, axis=-1, keepdims=True)).astype(bf16))
    out = dot(jnp.concatenate(weights, axis=0), v)
    total = jnp.zeros((n, D), f32)
    for h in range(HEADS):
        total = jnp.where(lane == h, out[h * n : (h + 1) * n], total)
    return total.astype(bf16)


def block(state, proj, spans, biases, wo, wu, wd):
    kept = []
    for (row, n), bias in zip(spans, biases):
        lo, hi = row - RIM, row + n + RIM
        kept.append(
            attend(proj[row : row + n, :D], proj[lo:hi, D : 2 * D], proj[lo:hi, 2 * D :], bias)
        )
    first = spans[0][0]
    last = spans[-1][0] + spans[-1][1]
    state = state[first:last] + dot(jnp.concatenate(kept, axis=0), wo)
    hidden = dot(norm(state), wu)
    gate, up = hidden[:, :FFH], hidden[:, FFH:]
    gated = (0.5 * gate * (1.0 + jnp.tanh(0.5 * gate)) * up).astype(bf16)
    return state + dot(gated, wd)


def project(rows, wq):
    return dot(norm(rows), wq).astype(bf16)


def tokens(atoms, match, counts, wt, wp):
    act = jnp.maximum(dot(atoms, wt), 0.0).astype(bf16)
    means = (dot(match, act) / counts).astype(bf16)
    return means, dot(means, wp).astype(bf16)


def matches(own_meta, right_meta):
    rel = jnp.concatenate([own_meta[0:1, :], right_meta[0:1, :RIM] + 2.0], axis=1)
    ids = lax.broadcasted_iota(jnp.int32, (16, ROWS + RIM), 0).astype(f32)
    match = jnp.where(ids == rel, 1.0, 0.0)
    return match.astype(bf16), jnp.maximum(jnp.sum(match, axis=-1, keepdims=True), 1.0)


def biases_of(metas, base, n_atoms):
    out = []
    for start, n, n_key in ((-RIM, RIM, 192), (0, ROWS, 256), (ROWS, ROWS, 256)):
        span = []
        for k in range(n // QBLK):
            at = (start + ROWS) // QBLK + k
            off = metas[at // 4][1:2, at % 4 : at % 4 + 1]
            span.append(window_bias(off, k, base + start, n_key, n_atoms))
        out.append(span)
    return out


SPANS1 = [(64, 64), (128, 128), (256, 128)]
SPANS2 = [(64, 128), (192, 64)]


def transform(pieces, own_proj, metas, base, n_atoms, wq, wo, wu, wd):
    left, own, right, far = pieces
    biases = biases_of(metas, base, n_atoms)
    rim = project(jnp.concatenate([left, right, far], axis=0), wq[0])
    proj = jnp.concatenate([rim[:ROWS], own_proj, rim[ROWS:]], axis=0)
    state = jnp.concatenate([left, own, right, far], axis=0)
    bias1 = [rows_of(biases[0], 192), rows_of(biases[1], 256), rows_of(biases[2], 256)]
    state = block(state, proj, SPANS1, bias1, wo[0], wu[0], wd[0])
    bias2 = [bias1[1], rows_of(biases[2][:2], 192)]
    proj = project(state, wq[1])
    return block(state, proj, SPANS2, bias2, wo[1], wu[1], wd[1])


def peers():
    every = [(dy, dz, dc) for dy in range(NY) for dz in range(-7, 9) for dc in range(2)]
    return sorted(every, key=lambda o: (-(min(o[0], NY - o[0]) + abs(o[1])), -o[2]))


def kernel(
    n_atoms,
    feats, tok, koff, w_qkv, w_out, w_up, w_down, w_tok, w_row, w_col,
    atom_out, single, rows_out, cols_out,
    halo, far, toks, offs, wq, wo, wu, wd, wt, wp, mine, rowbuf, colbuf,
    wsem, hsend, hrecv, rsend, rrecv, csend, crecv, around, beyond,
):
    wide, x = lax.axis_index("wide"), lax.axis_index("col")
    core = lax.rem(wide, 2)
    z = lax.rem(wide // 2, NZ)
    y = wide // (2 * NZ)
    me = wide * NX + x
    home = x == y

    def tell(sem, dev):
        pl.semaphore_signal(sem, inc=1, device_id=dev, device_id_type=MESH)

    def beside(d):
        return device(y, lax.rem(z + d + NZ, NZ), core, x)

    barrier = pltpu.get_barrier_semaphore()
    for step in (-1, 1, 2):
        tell(barrier, along(step))
    for d in NEAR:
        tell(barrier, beside(d))
    for xs in range(NX):
        for c in range(2):
            pl.when(jnp.logical_not(home & (core == c) & (xs == x)))(
                functools.partial(tell, barrier, device(x, z, c, xs))
            )
    for d in range(1, NX):
        tell(barrier, (wide, lax.rem(x + d, NX)))

    loads = []
    for n, (src, dst) in enumerate(
        [(feats, halo.at[1, pl.ds(0, ROWS)]), (tok, toks), (koff, offs),
         (w_qkv, wq), (w_out, wo), (w_up, wu), (w_down, wd), (w_tok, wt),
         (w_row, wp.at[:, pl.ds(0, D)]), (w_col, wp.at[:, pl.ds(D, D)])]
    ):
        loads.append(pltpu.make_async_copy(src, dst, wsem.at[n]))
        loads[-1].start()

    for load in loads[:3]:
        load.wait()
    row = lax.broadcasted_iota(jnp.int32, (16, D), 0)
    tok_rel = (toks[...] - 2 * me).astype(f32)
    off4 = jnp.concatenate(
        [offs[...].astype(f32)] + [jnp.zeros((1, 4), f32)] * (D // 4 - 1), axis=1
    )
    meta = jnp.where(row == 0, tok_rel, jnp.where(row == 1, off4, 0.0))
    halo[1, pl.ds(ROWS, 16)] = meta.astype(bf16)
    pl.semaphore_wait(barrier, 3 + 8 + 3 + len(NEAR) - home.astype(jnp.int32))

    sends = [
        pltpu.make_async_remote_copy(
            halo.at[1], halo.at[0], hsend.at[0], hrecv.at[0], along(1), MESH
        ),
        pltpu.make_async_remote_copy(
            halo.at[1], halo.at[2], hsend.at[1], hrecv.at[1], along(-1), MESH
        ),
        pltpu.make_async_remote_copy(
            halo.at[1, pl.ds(0, RIM)], far, hsend.at[2], hrecv.at[2], along(-2), MESH
        ),
    ]
    for s in sends:
        s.start()

    for d in NEAR:
        tell(around, beside(d))
    loads[3].wait()
    own = halo[1, pl.ds(0, ROWS)].astype(f32)
    own_proj = project(own, wq[0])
    for load in loads[4:]:
        load.wait()
    for s in sends:
        s.wait_recv()
    pl.semaphore_wait(around, len(NEAR))
    for d in (4, -4):
        tell(beyond, beside(d))

    metas = [halo[s, pl.ds(ROWS, 16)].astype(f32) for s in range(3)]
    pieces = [halo[0, pl.ds(0, ROWS)].astype(f32), own]
    pieces += [halo[2, pl.ds(0, ROWS)].astype(f32), far[...].astype(f32)]
    match, counts = matches(metas[1], metas[2])
    state = transform(pieces, own_proj, metas, me * ROWS, n_atoms, wq, wo, wu, wd)
    atoms = state.astype(bf16)
    means, proj = tokens(atoms, match, counts, wt[...], wp[...])
    mine[0] = proj[0:2, :D]
    mine[1] = proj[0:2, D:]
    pl.semaphore_wait(beyond, 2)

    def send_column(to):
        pltpu.make_async_remote_copy(
            mine.at[1], colbuf.at[wide % 32 * NX + x], csend, crecv, to, MESH
        ).start()

    for zd in range(NZ):
        for dy in (2, 1, 3, 0):
            for dc in (1, 0):
                to = device(lax.rem(y + dy, NY), zd, lax.rem(core + dc, 2), y)
                if dy or dc:
                    send_column(to)
                else:
                    pl.when(jnp.logical_not(home & (z == zd)))(functools.partial(send_column, to))
    pl.when(home)(
        pltpu.make_async_copy(mine.at[1], colbuf.at[wide % 32 * NX + x], crecv).start
    )
    for d in range(1, NX):
        pltpu.make_async_remote_copy(
            mine.at[0], rowbuf.at[x], rsend, rrecv, (wide, lax.rem(x + d, NX)), MESH
        ).start()
    rowbuf[pl.ds(x, 1)] = proj[0:2, :D].reshape(1, 2, D)
    atom_out[...] = atoms[:ROWS]
    single[...] = means[0:2]

    three = rowbuf.at[pl.ds(0, 3)]
    pltpu.make_async_copy(three, three, rrecv).wait()
    for s in range(NX):
        rows_out[pl.ds(2 * s, 2), :] = rowbuf[s].astype(f32)
    pltpu.make_async_copy(colbuf, colbuf, crecv).wait()
    for s in range(128):
        cols_out[pl.ds(2 * s, 2), :] = colbuf[s].astype(f32)
    for s in sends:
        s.wait_send()
    pltpu.make_async_copy(three, three, rsend).wait()
    less = colbuf.at[pl.ds(0, 127)]
    pl.when(home)(pltpu.make_async_copy(less, less, csend).wait)
    pl.when(jnp.logical_not(home))(pltpu.make_async_copy(colbuf, colbuf, csend).wait)


def finish(pair, rows, cols, atoms, means, pair_out, atom_out, single, sums, sem):
    copies = [
        pltpu.make_async_copy(atoms, atom_out, sem.at[0]),
        pltpu.make_async_copy(means, single, sem.at[1]),
    ]
    for copy in copies:
        copy.start()
    cols = cols[...]
    for r in range(8):
        sums[r] = ((pair[r].astype(f32) + rows[pl.ds(r, 1), :]) + cols).astype(bf16)
        copies.append(pltpu.make_async_copy(sums.at[r], pair_out.at[r], sem.at[r + 2]))
        copies[-1].start()
    for copy in copies:
        copy.wait()


def on_device(
    atom_feats, atom_token, key_offset, pair_in, w_qkv, w_out, w_up, w_down, w_tok, w_row, w_col
):
    vmem = pl.BlockSpec(memory_space=pltpu.VMEM)
    hbm = pl.BlockSpec(memory_space=pltpu.HBM)
    dma, flag = pltpu.SemaphoreType.DMA, pltpu.SemaphoreType.REGULAR
    atoms, means, row_vecs, col_vecs = pl.pallas_call(
        functools.partial(kernel, 512 * ROWS),
        out_shape=[
            jax.ShapeDtypeStruct((ROWS, D), bf16),
            jax.ShapeDtypeStruct((2, TOKC), bf16),
            jax.ShapeDtypeStruct((8, D), f32),
            jax.ShapeDtypeStruct((256, D), f32),
        ],
        in_specs=[hbm] * 10,
        out_specs=[vmem] * 4,
        scratch_shapes=[
            pltpu.VMEM((3, ROWS + 16, D), bf16),
            pltpu.VMEM((RIM, D), bf16),
            pltpu.VMEM((1, ROWS), jnp.int32),
            pltpu.VMEM((1, 4), jnp.int32),
            pltpu.VMEM((2, D, 3 * D), bf16),
            pltpu.VMEM((2, D, D), bf16),
            pltpu.VMEM((2, D, 2 * FFH), bf16),
            pltpu.VMEM((2, FFH, D), bf16),
            pltpu.VMEM((D, TOKC), bf16),
            pltpu.VMEM((TOKC, 2 * D), bf16),
            pltpu.VMEM((2, 2, D), bf16),
            pltpu.VMEM((NX, 2, D), bf16),
            pltpu.VMEM((128, 2, D), bf16),
            dma((10,)), dma((3,)), dma((3,)), dma, dma, dma, dma, flag, flag,
        ],
        compiler_params=pltpu.CompilerParams(
            collective_id=1, has_side_effects=True, vmem_limit_bytes=32 * 1024 * 1024
        ),
        name="atoms_tokens",
    )(
        *[
            pltpu.with_memory_space_constraint(a, pltpu.HBM)
            for a in (
                atom_feats, atom_token.reshape(1, ROWS), key_offset.reshape(1, 4),
                w_qkv, w_out, w_up, w_down, w_tok, w_row, w_col,
            )
        ]
    )
    pair_out, atom_out, single = pl.pallas_call(
        finish,
        out_shape=[
            jax.ShapeDtypeStruct(pair_in.shape, bf16),
            jax.ShapeDtypeStruct((ROWS, D), bf16),
            jax.ShapeDtypeStruct((2, TOKC), bf16),
        ],
        in_specs=[vmem] * 5,
        out_specs=[hbm] * 3,
        scratch_shapes=[pltpu.VMEM(pair_in.shape, bf16), dma((10,))],
        compiler_params=pltpu.CompilerParams(vmem_limit_bytes=16 * 1024 * 1024),
        name="pair_add",
    )(pair_in, row_vecs, col_vecs, atoms, means)
    return (atom_out, single, pair_out)


def solution(mesh):
    return jax.shard_map(
        on_device,
        mesh=mesh,
        in_specs=(
            P(("wide", "col"), None),
            P(("wide", "col")),
            P(("wide", "col")),
            P("wide", "col", None),
            P(), P(), P(), P(), P(), P(), P(),
        ),
        out_specs=(P(("wide", "col"), None), P(("wide", "col"), None), P("wide", "col", None)),
        check_vma=False,
    )
```

```python
import functools

import jax
import jax.numpy as jnp
from jax import lax
from jax.experimental import pallas as pl
from jax.experimental.pallas import tpu as pltpu
from jax.sharding import PartitionSpec as P

D = 128
HEADS = 4
HEAD = 32
FFH = 256
TOKC = 384
QBLK = 32
KWIN = 128
RIM = 64
ROWS = 128
NY, NZ, NX = 4, 16, 4
NEAR = (2, -2, 1, -1)
SCORE = 1.4426950408889634 / HEAD**0.5
NEG = -1e30
MESH = pl.DeviceIdType.MESH
f32, bf16 = jnp.float32, jnp.bfloat16


def device(y, z, core, x):
    return ((y * NZ + z) * 2 + core, x)


def along(step):
    at = lax.rem(lax.axis_index("wide") * NX + lax.axis_index("col") + step + 512, 512)
    return (at // NX, lax.rem(at, NX))


def dot(a, b):
    return jnp.dot(a, b, preferred_element_type=f32)


def normed_dot(v, w):
    c = v - jnp.mean(v, axis=-1, keepdims=True)
    scale = lax.rsqrt(jnp.mean(c * c, axis=-1, keepdims=True) + 1e-5)
    return dot(c.astype(bf16), w) * scale


def window_bias(offset, block, base, n_key, n_atoms):
    first = base - RIM
    at = base + block * QBLK
    outside = (at < 0) | (at >= n_atoms)
    floor = jnp.where(outside, -KWIN * 8, -first).astype(f32)
    ceil = jnp.where(outside, KWIN * 8, n_atoms - first).astype(f32)
    low = jnp.maximum(offset + float(block * QBLK), floor)
    high = jnp.minimum(offset + float(block * QBLK + KWIN), ceil)
    key = lax.broadcasted_iota(jnp.int32, (1, n_key), 1).astype(f32)
    return jnp.where((key >= low) & (key < high), 0.0, NEG)


def rows_of(blocks, n_key):
    return jnp.concatenate([jnp.broadcast_to(b[:, :n_key], (QBLK, n_key)) for b in blocks], axis=0)


def attend(q, k, v, bias):
    n = q.shape[0]
    lane = lax.broadcasted_iota(jnp.int32, (n, D), 1) // HEAD
    stacked = jnp.concatenate(
        [jnp.where(lane == h, q, jnp.zeros_like(q)) for h in range(HEADS)], axis=0
    )
    scores = lax.dot_general(stacked, k, (((1,), (1,)), ((), ())), preferred_element_type=f32)
    weights = []
    for h in range(HEADS):
        e = jnp.exp2(scores[h * n : (h + 1) * n] * SCORE + bias)
        weights.append((e / jnp.sum(e, axis=-1, keepdims=True)).astype(bf16))
    out = dot(jnp.concatenate(weights, axis=0), v)
    total = jnp.zeros((n, D), f32)
    for h in range(HEADS):
        total = jnp.where(lane == h, out[h * n : (h + 1) * n], total)
    return total.astype(bf16)


def block(state, proj, spans, biases, wo, wu, wd):
    kept = []
    for (row, n), bias in zip(spans, biases):
        lo, hi = row - RIM, row + n + RIM
        kept.append(
            attend(proj[row : row + n, :D], proj[lo:hi, D : 2 * D], proj[lo:hi, 2 * D :], bias)
        )
    first = spans[0][0]
    last = spans[-1][0] + spans[-1][1]
    state = state[first:last] + dot(jnp.concatenate(kept, axis=0), wo)
    hidden = normed_dot(state, wu)
    gate, up = hidden[:, :FFH], hidden[:, FFH:]
    gated = (0.5 * gate * (1.0 + jnp.tanh(0.5 * gate)) * up).astype(bf16)
    return state + dot(gated, wd)


def project(rows, wq):
    return normed_dot(rows, wq).astype(bf16)


def tokens(atoms, match, counts, wt, wp):
    act = jnp.maximum(dot(atoms, wt), 0.0).astype(bf16)
    means = (dot(match, act) / counts).astype(bf16)
    return means, dot(means, wp).astype(bf16)


def matches(own_meta, right_meta):
    rel = jnp.concatenate([own_meta[0:1, :], right_meta[0:1, :RIM] + 2.0], axis=1)
    ids = lax.broadcasted_iota(jnp.int32, (16, ROWS + RIM), 0).astype(f32)
    match = jnp.where(ids == rel, 1.0, 0.0)
    return match.astype(bf16), jnp.maximum(jnp.sum(match, axis=-1, keepdims=True), 1.0)


def biases_of(metas, base, n_atoms):
    out = []
    for start, n, n_key in ((-RIM, RIM, 192), (0, ROWS, 256), (ROWS, ROWS, 256)):
        span = []
        for k in range(n // QBLK):
            at = (start + ROWS) // QBLK + k
            off = metas[at // 4][1:2, at % 4 : at % 4 + 1]
            span.append(window_bias(off, k, base + start, n_key, n_atoms))
        out.append(span)
    return out


SPANS1 = [(64, 64), (128, 128), (256, 128)]
SPANS2 = [(64, 128), (192, 64)]


def transform(pieces, own_proj, metas, base, n_atoms, wq, wo, wu, wd, between):
    left, own, right, far = pieces
    biases = biases_of(metas, base, n_atoms)
    rim = project(jnp.concatenate([left, right, far], axis=0), wq[0])
    proj = jnp.concatenate([rim[:ROWS], own_proj, rim[ROWS:]], axis=0)
    state = jnp.concatenate([left, own, right, far], axis=0)
    bias1 = [rows_of(biases[0], 192), rows_of(biases[1], 256), rows_of(biases[2], 256)]
    state = block(state, proj, SPANS1, bias1, wo[0], wu[0], wd[0])
    between()
    bias2 = [bias1[1], rows_of(biases[2][:2], 192)]
    proj = project(state, wq[1])
    return block(state, proj, SPANS2, bias2, wo[1], wu[1], wd[1])


def peers():
    every = [(dy, dz, dc) for dy in range(NY) for dz in range(-7, 9) for dc in range(2)]
    return sorted(every, key=lambda o: (-(min(o[0], NY - o[0]) + abs(o[1])), -o[2]))


def kernel(
    n_atoms,
    feats, tok, koff, w_qkv, w_out, w_up, w_down, w_tok, w_row, w_col,
    atom_out, single, rows_out, cols_out,
    halo, far, toks, offs, wq, wo, wu, wd, wt, wp, mine, rowbuf, colbuf,
    wsem, hsend, hrecv, rsend, rrecv, csend, crecv, around, beyond, rest,
):
    wide, x = lax.axis_index("wide"), lax.axis_index("col")
    core = lax.rem(wide, 2)
    z = lax.rem(wide // 2, NZ)
    y = wide // (2 * NZ)
    me = wide * NX + x
    home = x == y

    def tell(sem, dev):
        pl.semaphore_signal(sem, inc=1, device_id=dev, device_id_type=MESH)

    def beside(d):
        return device(y, lax.rem(z + d + NZ, NZ), core, x)

    barrier = pltpu.get_barrier_semaphore()
    for step in (-1, 1, 2):
        tell(barrier, along(step))
    for d in NEAR:
        tell(barrier, beside(d))
    for xs in range(NX):
        for c in range(2):
            pl.when(jnp.logical_not(home & (core == c) & (xs == x)))(
                functools.partial(tell, barrier, device(x, z, c, xs))
            )
    for d in range(1, NX):
        tell(barrier, (wide, lax.rem(x + d, NX)))

    loads = []
    for n, (src, dst) in enumerate(
        [(feats, halo.at[1, pl.ds(0, ROWS)]), (tok, toks), (koff, offs),
         (w_qkv, wq), (w_out, wo), (w_up, wu), (w_down, wd), (w_tok, wt),
         (w_row, wp.at[:, pl.ds(0, D)]), (w_col, wp.at[:, pl.ds(D, D)])]
    ):
        loads.append(pltpu.make_async_copy(src, dst, wsem.at[n]))
        loads[-1].start()

    for load in loads[:3]:
        load.wait()
    row = lax.broadcasted_iota(jnp.int32, (16, D), 0)
    tok_rel = (toks[...] - 2 * me).astype(f32)
    off4 = jnp.concatenate(
        [offs[...].astype(f32)] + [jnp.zeros((1, 4), f32)] * (D // 4 - 1), axis=1
    )
    meta = jnp.where(row == 0, tok_rel, jnp.where(row == 1, off4, 0.0))
    halo[1, pl.ds(ROWS, 16)] = meta.astype(bf16)
    pl.semaphore_wait(barrier, 3 + 8 + 3 + len(NEAR) - home.astype(jnp.int32))

    sends = [
        pltpu.make_async_remote_copy(
            halo.at[1], halo.at[0], hsend.at[0], hrecv.at[0], along(1), MESH
        ),
        pltpu.make_async_remote_copy(
            halo.at[1], halo.at[2], hsend.at[1], hrecv.at[1], along(-1), MESH
        ),
        pltpu.make_async_remote_copy(
            halo.at[1, pl.ds(0, RIM)], far, hsend.at[2], hrecv.at[2], along(-2), MESH
        ),
    ]
    for s in sends:
        s.start()

    for d in NEAR:
        tell(around, beside(d))
    loads[3].wait()
    own = halo[1, pl.ds(0, ROWS)].astype(f32)
    own_proj = project(own, wq[0])
    for load in loads[4:]:
        load.wait()
    pl.semaphore_wait(around, len(NEAR))
    for d in (4, -4):
        tell(beyond, beside(d))
    for s in sends:
        s.wait_recv()

    metas = [halo[s, pl.ds(ROWS, 16)].astype(f32) for s in range(3)]
    pieces = [halo[0, pl.ds(0, ROWS)].astype(f32), own]
    pieces += [halo[2, pl.ds(0, ROWS)].astype(f32), far[...].astype(f32)]
    match, counts = matches(metas[1], metas[2])

    def pass_on():
        pl.semaphore_wait(beyond, 2)
        for d in (2, -2):
            tell(rest, beside(d))

    state = transform(pieces, own_proj, metas, me * ROWS, n_atoms, wq, wo, wu, wd, pass_on)
    atoms = state.astype(bf16)
    means, proj = tokens(atoms, match, counts, wt[...], wp[...])
    mine[0] = proj[0:2, :D]
    mine[1] = proj[0:2, D:]
    pl.semaphore_wait(rest, 2)

    def send_column(to):
        pltpu.make_async_remote_copy(
            mine.at[1], colbuf.at[wide % 32 * NX + x], csend, crecv, to, MESH
        ).start()

    for zd in range(NZ):
        for dy in (2, 1, 3, 0):
            for dc in (1, 0):
                to = device(lax.rem(y + dy, NY), zd, lax.rem(core + dc, 2), y)
                if dy or dc:
                    send_column(to)
                else:
                    pl.when(jnp.logical_not(home & (z == zd)))(functools.partial(send_column, to))
    pl.when(home)(
        pltpu.make_async_copy(mine.at[1], colbuf.at[wide % 32 * NX + x], crecv).start
    )
    for d in range(1, NX):
        pltpu.make_async_remote_copy(
            mine.at[0], rowbuf.at[x], rsend, rrecv, (wide, lax.rem(x + d, NX)), MESH
        ).start()
    rowbuf[pl.ds(x, 1)] = proj[0:2, :D].reshape(1, 2, D)
    atom_out[...] = atoms[:ROWS]
    single[...] = means[0:2]

    three = rowbuf.at[pl.ds(0, 3)]
    pltpu.make_async_copy(three, three, rrecv).wait()
    for s in range(NX):
        rows_out[pl.ds(2 * s, 2), :] = rowbuf[s].astype(f32)
    pltpu.make_async_copy(colbuf, colbuf, crecv).wait()
    for s in range(128):
        cols_out[pl.ds(2 * s, 2), :] = colbuf[s].astype(f32)
    for s in sends:
        s.wait_send()
    pltpu.make_async_copy(three, three, rsend).wait()
    less = colbuf.at[pl.ds(0, 127)]
    pl.when(home)(pltpu.make_async_copy(less, less, csend).wait)
    pl.when(jnp.logical_not(home))(pltpu.make_async_copy(colbuf, colbuf, csend).wait)


def finish(pair, rows, cols, atoms, means, pair_out, atom_out, single, sums, sem):
    copies = [
        pltpu.make_async_copy(atoms, atom_out, sem.at[0]),
        pltpu.make_async_copy(means, single, sem.at[1]),
    ]
    for copy in copies:
        copy.start()
    cols = cols[...]
    for r in range(8):
        sums[r] = ((pair[r].astype(f32) + rows[pl.ds(r, 1), :]) + cols).astype(bf16)
        copies.append(pltpu.make_async_copy(sums.at[r], pair_out.at[r], sem.at[r + 2]))
        copies[-1].start()
    for copy in copies:
        copy.wait()


def on_device(
    atom_feats, atom_token, key_offset, pair_in, w_qkv, w_out, w_up, w_down, w_tok, w_row, w_col
):
    vmem = pl.BlockSpec(memory_space=pltpu.VMEM)
    hbm = pl.BlockSpec(memory_space=pltpu.HBM)
    dma, flag = pltpu.SemaphoreType.DMA, pltpu.SemaphoreType.REGULAR
    atoms, means, row_vecs, col_vecs = pl.pallas_call(
        functools.partial(kernel, 512 * ROWS),
        out_shape=[
            jax.ShapeDtypeStruct((ROWS, D), bf16),
            jax.ShapeDtypeStruct((2, TOKC), bf16),
            jax.ShapeDtypeStruct((8, D), f32),
            jax.ShapeDtypeStruct((256, D), f32),
        ],
        in_specs=[hbm] * 10,
        out_specs=[vmem] * 4,
        scratch_shapes=[
            pltpu.VMEM((3, ROWS + 16, D), bf16),
            pltpu.VMEM((RIM, D), bf16),
            pltpu.VMEM((1, ROWS), jnp.int32),
            pltpu.VMEM((1, 4), jnp.int32),
            pltpu.VMEM((2, D, 3 * D), bf16),
            pltpu.VMEM((2, D, D), bf16),
            pltpu.VMEM((2, D, 2 * FFH), bf16),
            pltpu.VMEM((2, FFH, D), bf16),
            pltpu.VMEM((D, TOKC), bf16),
            pltpu.VMEM((TOKC, 2 * D), bf16),
            pltpu.VMEM((2, 2, D), bf16),
            pltpu.VMEM((NX, 2, D), bf16),
            pltpu.VMEM((128, 2, D), bf16),
            dma((10,)), dma((3,)), dma((3,)), dma, dma, dma, dma, flag, flag, flag,
        ],
        compiler_params=pltpu.CompilerParams(
            collective_id=1, has_side_effects=True, vmem_limit_bytes=32 * 1024 * 1024
        ),
        name="atoms_tokens",
    )(
        *[
            pltpu.with_memory_space_constraint(a, pltpu.HBM)
            for a in (
                atom_feats, atom_token.reshape(1, ROWS), key_offset.reshape(1, 4),
                w_qkv, w_out, w_up, w_down, w_tok, w_row, w_col,
            )
        ]
    )
    pair_out, atom_out, single = pl.pallas_call(
        finish,
        out_shape=[
            jax.ShapeDtypeStruct(pair_in.shape, bf16),
            jax.ShapeDtypeStruct((ROWS, D), bf16),
            jax.ShapeDtypeStruct((2, TOKC), bf16),
        ],
        in_specs=[vmem] * 5,
        out_specs=[hbm] * 3,
        scratch_shapes=[pltpu.VMEM(pair_in.shape, bf16), dma((10,))],
        compiler_params=pltpu.CompilerParams(vmem_limit_bytes=16 * 1024 * 1024),
        name="pair_add",
    )(pair_in, row_vecs, col_vecs, atoms, means)
    return (atom_out, single, pair_out)


def solution(mesh):
    return jax.shard_map(
        on_device,
        mesh=mesh,
        in_specs=(
            P(("wide", "col"), None),
            P(("wide", "col")),
            P(("wide", "col")),
            P("wide", "col", None),
            P(), P(), P(), P(), P(), P(), P(),
        ),
        out_specs=(P(("wide", "col"), None), P(("wide", "col"), None), P("wide", "col", None)),
        check_vma=False,
    )
```

```python
import functools

import jax
import jax.numpy as jnp
from jax import lax
from jax.experimental import pallas as pl
from jax.experimental.pallas import tpu as pltpu
from jax.sharding import PartitionSpec as P

D = 128
HEADS = 4
HEAD = 32
FFH = 256
TOKC = 384
QBLK = 32
KWIN = 128
RIM = 64
ROWS = 128
NY, NZ, NX = 4, 16, 4
NEAR = (2, -2, 1, -1)
SCORE = 1.4426950408889634 / HEAD**0.5
NEG = -1e30
MESH = pl.DeviceIdType.MESH
f32, bf16 = jnp.float32, jnp.bfloat16


def device(y, z, core, x):
    return ((y * NZ + z) * 2 + core, x)


def along(step):
    at = lax.rem(lax.axis_index("wide") * NX + lax.axis_index("col") + step + 512, 512)
    return (at // NX, lax.rem(at, NX))


def dot(a, b):
    return jnp.dot(a, b, preferred_element_type=f32)


def normed_dot(v, w):
    c = v - jnp.mean(v, axis=-1, keepdims=True)
    scale = lax.rsqrt(jnp.mean(c * c, axis=-1, keepdims=True) + 1e-5)
    return dot(c.astype(bf16), w) * scale


def window_bias(offset, block, base, n_key, n_atoms):
    first = base - RIM
    at = base + block * QBLK
    outside = (at < 0) | (at >= n_atoms)
    floor = jnp.where(outside, -KWIN * 8, -first).astype(f32)
    ceil = jnp.where(outside, KWIN * 8, n_atoms - first).astype(f32)
    low = jnp.maximum(offset + float(block * QBLK), floor)
    high = jnp.minimum(offset + float(block * QBLK + KWIN), ceil)
    key = lax.broadcasted_iota(jnp.int32, (1, n_key), 1).astype(f32)
    return jnp.where((key >= low) & (key < high), 0.0, NEG)


def rows_of(blocks, n_key):
    return jnp.concatenate([jnp.broadcast_to(b[:, :n_key], (QBLK, n_key)) for b in blocks], axis=0)


def attend(q, k, v, bias):
    n = q.shape[0]
    lane = lax.broadcasted_iota(jnp.int32, (n, D), 1) // HEAD
    stacked = jnp.concatenate(
        [jnp.where(lane == h, q, jnp.zeros_like(q)) for h in range(HEADS)], axis=0
    )
    scores = lax.dot_general(stacked, k, (((1,), (1,)), ((), ())), preferred_element_type=f32)
    weights = []
    for h in range(HEADS):
        e = jnp.exp2(scores[h * n : (h + 1) * n] * SCORE + bias)
        weights.append((e / jnp.sum(e, axis=-1, keepdims=True)).astype(bf16))
    out = dot(jnp.concatenate(weights, axis=0), v)
    total = jnp.zeros((n, D), f32)
    for h in range(HEADS):
        total = jnp.where(lane == h, out[h * n : (h + 1) * n], total)
    return total.astype(bf16)


def block(state, proj, spans, biases, wo, wu, wd):
    kept = []
    for (row, n), bias in zip(spans, biases):
        lo, hi = row - RIM, row + n + RIM
        kept.append(
            attend(proj[row : row + n, :D], proj[lo:hi, D : 2 * D], proj[lo:hi, 2 * D :], bias)
        )
    first = spans[0][0]
    last = spans[-1][0] + spans[-1][1]
    state = state[first:last] + dot(jnp.concatenate(kept, axis=0), wo)
    hidden = normed_dot(state, wu)
    gate, up = hidden[:, :FFH], hidden[:, FFH:]
    gated = (0.5 * gate * (1.0 + jnp.tanh(0.5 * gate)) * up).astype(bf16)
    return state + dot(gated, wd)


def project(rows, wq):
    return normed_dot(rows, wq).astype(bf16)


def tokens(atoms, match, counts, wt, wp):
    act = jnp.maximum(dot(atoms, wt), 0.0).astype(bf16)
    means = (dot(match, act) / counts).astype(bf16)
    return means, dot(means, wp).astype(bf16)


def matches(own_meta, right_meta):
    rel = jnp.concatenate([own_meta[0:1, :], right_meta[0:1, :RIM] + 2.0], axis=1)
    ids = lax.broadcasted_iota(jnp.int32, (16, ROWS + RIM), 0).astype(f32)
    match = jnp.where(ids == rel, 1.0, 0.0)
    return match.astype(bf16), jnp.maximum(jnp.sum(match, axis=-1, keepdims=True), 1.0)


def biases_of(metas, base, n_atoms):
    out = []
    for start, n, n_key in ((-RIM, RIM, 192), (0, ROWS, 256), (ROWS, ROWS, 256)):
        span = []
        for k in range(n // QBLK):
            at = (start + ROWS) // QBLK + k
            off = metas[at // 4][1:2, at % 4 : at % 4 + 1]
            span.append(window_bias(off, k, base + start, n_key, n_atoms))
        out.append(span)
    return out


SPANS1 = [(64, 64), (128, 128), (256, 128)]
SPANS2 = [(64, 128), (192, 64)]


def transform(pieces, own_proj, metas, base, n_atoms, wq, wo, wu, wd, between):
    left, own, right, far = pieces
    biases = biases_of(metas, base, n_atoms)
    rim = project(jnp.concatenate([left, right, far], axis=0), wq[0])
    proj = jnp.concatenate([rim[:ROWS], own_proj, rim[ROWS:]], axis=0)
    state = jnp.concatenate([left, own, right, far], axis=0)
    bias1 = [rows_of(biases[0], 192), rows_of(biases[1], 256), rows_of(biases[2], 256)]
    state = block(state, proj, SPANS1, bias1, wo[0], wu[0], wd[0])
    between()
    bias2 = [bias1[1], rows_of(biases[2][:2], 192)]
    proj = project(state, wq[1])
    return block(state, proj, SPANS2, bias2, wo[1], wu[1], wd[1])


def peers():
    every = [(dy, dz, dc) for dy in range(NY) for dz in range(-7, 9) for dc in range(2)]
    return sorted(every, key=lambda o: (-(min(o[0], NY - o[0]) + abs(o[1])), -o[2]))


def kernel(
    n_atoms,
    feats, tok, koff, w_qkv, w_out, w_up, w_down, w_tok, w_row, w_col,
    atom_out, single, rows_out, cols_out,
    halo, far, toks, offs, wq, wo, wu, wd, wt, wp, mine, rowbuf, colbuf,
    wsem, hsend, hrecv, rsend, rrecv, csend, crecv, around, beyond, rest,
):
    wide, x = lax.axis_index("wide"), lax.axis_index("col")
    core = lax.rem(wide, 2)
    z = lax.rem(wide // 2, NZ)
    y = wide // (2 * NZ)
    me = wide * NX + x
    home = x == y

    def tell(sem, dev):
        pl.semaphore_signal(sem, inc=1, device_id=dev, device_id_type=MESH)

    def beside(d):
        return device(y, lax.rem(z + d + NZ, NZ), core, x)

    barrier = pltpu.get_barrier_semaphore()
    for step in (-1, 1, 2):
        tell(barrier, along(step))
    for d in NEAR:
        tell(barrier, beside(d))
    for xs in range(NX):
        for c in range(2):
            pl.when(jnp.logical_not(home & (core == c) & (xs == x)))(
                functools.partial(tell, barrier, device(x, z, c, xs))
            )
    for d in range(1, NX):
        tell(barrier, (wide, lax.rem(x + d, NX)))

    loads = []
    for n, (src, dst) in enumerate(
        [(feats, halo.at[1, pl.ds(0, ROWS)]), (tok, toks), (koff, offs),
         (w_qkv, wq), (w_out, wo), (w_up, wu), (w_down, wd), (w_tok, wt),
         (w_row, wp.at[:, pl.ds(0, D)]), (w_col, wp.at[:, pl.ds(D, D)])]
    ):
        loads.append(pltpu.make_async_copy(src, dst, wsem.at[n]))
        loads[-1].start()

    for load in loads[:3]:
        load.wait()
    row = lax.broadcasted_iota(jnp.int32, (16, D), 0)
    tok_rel = (toks[...] - 2 * me).astype(f32)
    off4 = jnp.concatenate(
        [offs[...].astype(f32)] + [jnp.zeros((1, 4), f32)] * (D // 4 - 1), axis=1
    )
    meta = jnp.where(row == 0, tok_rel, jnp.where(row == 1, off4, 0.0))
    halo[1, pl.ds(ROWS, 16)] = meta.astype(bf16)
    pl.semaphore_wait(barrier, 3 + 8 + 3 + len(NEAR) - home.astype(jnp.int32))

    sends = [
        pltpu.make_async_remote_copy(
            halo.at[1], halo.at[0], hsend.at[0], hrecv.at[0], along(1), MESH
        ),
        pltpu.make_async_remote_copy(
            halo.at[1], halo.at[2], hsend.at[1], hrecv.at[1], along(-1), MESH
        ),
        pltpu.make_async_remote_copy(
            halo.at[1, pl.ds(0, RIM)], far, hsend.at[2], hrecv.at[2], along(-2), MESH
        ),
    ]
    for s in (sends[2], sends[0], sends[1]):
        s.start()

    for d in NEAR:
        tell(around, beside(d))
    loads[3].wait()
    own = halo[1, pl.ds(0, ROWS)].astype(f32)
    own_proj = project(own, wq[0])
    for load in loads[4:]:
        load.wait()
    pl.semaphore_wait(around, len(NEAR))
    for d in (4, -4):
        tell(beyond.at[0 if d > 0 else 1], beside(d))
    for s in sends:
        s.wait_recv()

    metas = [halo[s, pl.ds(ROWS, 16)].astype(f32) for s in range(3)]
    pieces = [halo[0, pl.ds(0, ROWS)].astype(f32), own]
    pieces += [halo[2, pl.ds(0, ROWS)].astype(f32), far[...].astype(f32)]
    match, counts = matches(metas[1], metas[2])

    near_side = (z > NZ // 2).astype(jnp.int32)

    def pass_on(which):
        pl.semaphore_wait(beyond.at[which], 1)
        tell(rest.at[which], beside(2 - 4 * which))

    state = transform(pieces, own_proj, metas, me * ROWS, n_atoms, wq, wo, wu, wd, functools.partial(pass_on, near_side))
    atoms = state.astype(bf16)
    means, proj = tokens(atoms, match, counts, wt[...], wp[...])
    mine[0] = proj[0:2, :D]
    mine[1] = proj[0:2, D:]
    slot = lax.rem(wide, 32) * NX + x

    def send_columns(zd, _, part):
        ahead = lax.rem((z - zd) * (1 - 2 * near_side) + NZ, NZ)
        beside_me = (ahead <= 2) | (ahead >= NZ - 2)
        this = (beside_me, (ahead > 2) & (ahead <= 8), (ahead > 8) & (ahead < NZ - 2))[part]

        @pl.when(this)
        def _():
            for dy in (2, 1, 3, 0):
                for dc in (1, 0):
                    to = device(lax.rem(y + dy, NY), zd, lax.rem(core + dc, 2), y)
                    copy = pltpu.make_async_remote_copy(
                        mine.at[1], colbuf.at[slot], csend, crecv, to, MESH
                    )
                    if dy or dc:
                        copy.start()
                    else:
                        pl.when(jnp.logical_not(home & (z == zd)))(copy.start)

        return 0

    def send_part(part):
        lax.fori_loop(0, NZ, functools.partial(send_columns, part=part), 0)

    pass_on(1 - near_side)
    pl.when(z < 4)(functools.partial(send_part, 0))
    pl.semaphore_wait(rest.at[near_side], 1)
    send_part(1)
    pl.when(z >= 4)(functools.partial(send_part, 0))
    pl.semaphore_wait(rest.at[1 - near_side], 1)
    send_part(2)
    pl.when(home)(
        pltpu.make_async_copy(mine.at[1], colbuf.at[slot], crecv).start
    )
    for d in range(1, NX):
        pltpu.make_async_remote_copy(
            mine.at[0], rowbuf.at[x], rsend, rrecv, (wide, lax.rem(x + d, NX)), MESH
        ).start()
    rowbuf[pl.ds(x, 1)] = proj[0:2, :D].reshape(1, 2, D)
    atom_out[...] = atoms[:ROWS]
    single[...] = means[0:2]

    three = rowbuf.at[pl.ds(0, 3)]
    pltpu.make_async_copy(three, three, rrecv).wait()
    for s in range(NX):
        rows_out[pl.ds(2 * s, 2), :] = rowbuf[s].astype(f32)
    pltpu.make_async_copy(colbuf, colbuf, crecv).wait()
    for s in range(128):
        cols_out[pl.ds(2 * s, 2), :] = colbuf[s].astype(f32)
    for s in sends:
        s.wait_send()
    pltpu.make_async_copy(three, three, rsend).wait()
    less = colbuf.at[pl.ds(0, 127)]
    pl.when(home)(pltpu.make_async_copy(less, less, csend).wait)
    pl.when(jnp.logical_not(home))(pltpu.make_async_copy(colbuf, colbuf, csend).wait)


def finish(pair, rows, cols, atoms, means, pair_out, atom_out, single, sums, sem):
    copies = [
        pltpu.make_async_copy(atoms, atom_out, sem.at[0]),
        pltpu.make_async_copy(means, single, sem.at[1]),
    ]
    for copy in copies:
        copy.start()
    cols = cols[...]
    for r in range(8):
        sums[r] = ((pair[r].astype(f32) + rows[pl.ds(r, 1), :]) + cols).astype(bf16)
        copies.append(pltpu.make_async_copy(sums.at[r], pair_out.at[r], sem.at[r + 2]))
        copies[-1].start()
    for copy in copies:
        copy.wait()


def on_device(
    atom_feats, atom_token, key_offset, pair_in, w_qkv, w_out, w_up, w_down, w_tok, w_row, w_col
):
    vmem = pl.BlockSpec(memory_space=pltpu.VMEM)
    hbm = pl.BlockSpec(memory_space=pltpu.HBM)
    dma, flag = pltpu.SemaphoreType.DMA, pltpu.SemaphoreType.REGULAR
    atoms, means, row_vecs, col_vecs = pl.pallas_call(
        functools.partial(kernel, 512 * ROWS),
        out_shape=[
            jax.ShapeDtypeStruct((ROWS, D), bf16),
            jax.ShapeDtypeStruct((2, TOKC), bf16),
            jax.ShapeDtypeStruct((8, D), f32),
            jax.ShapeDtypeStruct((256, D), f32),
        ],
        in_specs=[hbm] * 10,
        out_specs=[vmem] * 4,
        scratch_shapes=[
            pltpu.VMEM((3, ROWS + 16, D), bf16),
            pltpu.VMEM((RIM, D), bf16),
            pltpu.VMEM((1, ROWS), jnp.int32),
            pltpu.VMEM((1, 4), jnp.int32),
            pltpu.VMEM((2, D, 3 * D), bf16),
            pltpu.VMEM((2, D, D), bf16),
            pltpu.VMEM((2, D, 2 * FFH), bf16),
            pltpu.VMEM((2, FFH, D), bf16),
            pltpu.VMEM((D, TOKC), bf16),
            pltpu.VMEM((TOKC, 2 * D), bf16),
            pltpu.VMEM((2, 2, D), bf16),
            pltpu.VMEM((NX, 2, D), bf16),
            pltpu.VMEM((128, 2, D), bf16),
            dma((10,)), dma((3,)), dma((3,)), dma, dma, dma, dma, flag, flag((2,)), flag((2,)),
        ],
        compiler_params=pltpu.CompilerParams(
            collective_id=1, has_side_effects=True, vmem_limit_bytes=32 * 1024 * 1024
        ),
        name="atoms_tokens",
    )(
        *[
            pltpu.with_memory_space_constraint(a, pltpu.HBM)
            for a in (
                atom_feats, atom_token.reshape(1, ROWS), key_offset.reshape(1, 4),
                w_qkv, w_out, w_up, w_down, w_tok, w_row, w_col,
            )
        ]
    )
    pair_out, atom_out, single = pl.pallas_call(
        finish,
        out_shape=[
            jax.ShapeDtypeStruct(pair_in.shape, bf16),
            jax.ShapeDtypeStruct((ROWS, D), bf16),
            jax.ShapeDtypeStruct((2, TOKC), bf16),
        ],
        in_specs=[vmem] * 5,
        out_specs=[hbm] * 3,
        scratch_shapes=[pltpu.VMEM(pair_in.shape, bf16), dma((10,))],
        compiler_params=pltpu.CompilerParams(vmem_limit_bytes=16 * 1024 * 1024),
        name="pair_add",
    )(pair_in, row_vecs, col_vecs, atoms, means)
    return (atom_out, single, pair_out)


def solution(mesh):
    return jax.shard_map(
        on_device,
        mesh=mesh,
        in_specs=(
            P(("wide", "col"), None),
            P(("wide", "col")),
            P(("wide", "col")),
            P("wide", "col", None),
            P(), P(), P(), P(), P(), P(), P(),
        ),
        out_specs=(P(("wide", "col"), None), P(("wide", "col"), None), P("wide", "col", None)),
        check_vma=False,
    )
```

```python
import functools

import jax
import jax.numpy as jnp
from jax import lax
from jax.experimental import pallas as pl
from jax.experimental.pallas import tpu as pltpu
from jax.sharding import PartitionSpec as P

D = 128
HEADS = 4
HEAD = 32
FFH = 256
TOKC = 384
QBLK = 32
KWIN = 128
RIM = 64
ROWS = 128
NY, NZ, NX = 4, 16, 4
NEAR = (2, -2, 1, -1)
SCORE = 1.4426950408889634 / HEAD**0.5
NEG = -1e30
MESH = pl.DeviceIdType.MESH
f32, bf16 = jnp.float32, jnp.bfloat16


def device(y, z, core, x):
    return ((y * NZ + z) * 2 + core, x)


def along(step):
    at = lax.rem(lax.axis_index("wide") * NX + lax.axis_index("col") + step + 512, 512)
    return (at // NX, lax.rem(at, NX))


def dot(a, b):
    return jnp.dot(a, b, preferred_element_type=f32)


def normed_dot(v, w):
    c = v - jnp.mean(v, axis=-1, keepdims=True)
    scale = lax.rsqrt(jnp.mean(c * c, axis=-1, keepdims=True) + 1e-5)
    return dot(c.astype(bf16), w) * scale


def window_bias(offset, block, base, n_key, n_atoms):
    first = base - RIM
    at = base + block * QBLK
    outside = (at < 0) | (at >= n_atoms)
    floor = jnp.where(outside, -KWIN * 8, -first).astype(f32)
    ceil = jnp.where(outside, KWIN * 8, n_atoms - first).astype(f32)
    low = jnp.maximum(offset + float(block * QBLK), floor)
    high = jnp.minimum(offset + float(block * QBLK + KWIN), ceil)
    key = lax.broadcasted_iota(jnp.int32, (1, n_key), 1).astype(f32)
    return jnp.where((key >= low) & (key < high), 0.0, NEG)


def rows_of(blocks, n_key):
    return jnp.concatenate([jnp.broadcast_to(b[:, :n_key], (QBLK, n_key)) for b in blocks], axis=0)


def attend(q, k, v, bias):
    n = q.shape[0]
    lane = lax.broadcasted_iota(jnp.int32, (n, D), 1) // HEAD
    stacked = jnp.concatenate(
        [jnp.where(lane == h, q, jnp.zeros_like(q)) for h in range(HEADS)], axis=0
    )
    scores = lax.dot_general(stacked, k, (((1,), (1,)), ((), ())), preferred_element_type=f32)
    weights = []
    for h in range(HEADS):
        e = jnp.exp2(scores[h * n : (h + 1) * n] * SCORE + bias)
        weights.append((e / jnp.sum(e, axis=-1, keepdims=True)).astype(bf16))
    out = dot(jnp.concatenate(weights, axis=0), v)
    total = jnp.zeros((n, D), f32)
    for h in range(HEADS):
        total = jnp.where(lane == h, out[h * n : (h + 1) * n], total)
    return total.astype(bf16)


def block(state, proj, spans, biases, wo, wu, wd):
    kept = []
    for (row, n), bias in zip(spans, biases):
        lo, hi = row - RIM, row + n + RIM
        kept.append(
            attend(proj[row : row + n, :D], proj[lo:hi, D : 2 * D], proj[lo:hi, 2 * D :], bias)
        )
    first = spans[0][0]
    last = spans[-1][0] + spans[-1][1]
    state = state[first:last] + dot(jnp.concatenate(kept, axis=0), wo)
    hidden = normed_dot(state, wu)
    gate, up = hidden[:, :FFH], hidden[:, FFH:]
    gated = (0.5 * gate * (1.0 + jnp.tanh(0.5 * gate)) * up).astype(bf16)
    return state + dot(gated, wd)


def project(rows, wq):
    return normed_dot(rows, wq).astype(bf16)


def tokens(atoms, match, counts, wt, wp):
    act = jnp.maximum(dot(atoms, wt), 0.0).astype(bf16)
    means = (dot(match, act) / counts).astype(bf16)
    return means, dot(means, wp).astype(bf16)


def matches(own_meta, right_meta):
    rel = jnp.concatenate([own_meta[0:1, :], right_meta[0:1, :RIM] + 2.0], axis=1)
    ids = lax.broadcasted_iota(jnp.int32, (16, ROWS + RIM), 0).astype(f32)
    match = jnp.where(ids == rel, 1.0, 0.0)
    return match.astype(bf16), jnp.maximum(jnp.sum(match, axis=-1, keepdims=True), 1.0)


def biases_of(metas, base, n_atoms):
    out = []
    for start, n, n_key in ((-RIM, RIM, 192), (0, ROWS, 256), (ROWS, ROWS, 256)):
        span = []
        for k in range(n // QBLK):
            at = (start + ROWS) // QBLK + k
            off = metas[at // 4][1:2, at % 4 : at % 4 + 1]
            span.append(window_bias(off, k, base + start, n_key, n_atoms))
        out.append(span)
    return out


SPANS1 = [(64, 64), (128, 128), (256, 128)]
SPANS2 = [(64, 128), (192, 64)]


def transform(pieces, own_proj, metas, base, n_atoms, wq, wo, wu, wd, between):
    left, own, right, far = pieces
    biases = biases_of(metas, base, n_atoms)
    rim = project(jnp.concatenate([left, right, far], axis=0), wq[0])
    proj = jnp.concatenate([rim[:ROWS], own_proj, rim[ROWS:]], axis=0)
    state = jnp.concatenate([left, own, right, far], axis=0)
    bias1 = [rows_of(biases[0], 192), rows_of(biases[1], 256), rows_of(biases[2], 256)]
    state = block(state, proj, SPANS1, bias1, wo[0], wu[0], wd[0])
    between()
    bias2 = [bias1[1], rows_of(biases[2][:2], 192)]
    proj = project(state, wq[1])
    return block(state, proj, SPANS2, bias2, wo[1], wu[1], wd[1])


def kernel(
    n_atoms,
    feats, tok, koff, w_qkv, w_out, w_up, w_down, w_tok, w_row, w_col,
    atom_out, single, rows_out, cols_out,
    halo, far, toks, offs, wq, wo, wu, wd, wt, wp, mine, rowbuf, colbuf,
    wsem, hsend, hrecv, rsend, rrecv, csend, crecv, around, beyond, rest,
):
    wide, x = lax.axis_index("wide"), lax.axis_index("col")
    core = lax.rem(wide, 2)
    z = lax.rem(wide // 2, NZ)
    y = wide // (2 * NZ)
    me = wide * NX + x
    home = x == y

    def tell(sem, dev):
        pl.semaphore_signal(sem, inc=1, device_id=dev, device_id_type=MESH)

    def beside(d):
        return device(y, lax.rem(z + d + NZ, NZ), core, x)

    barrier = pltpu.get_barrier_semaphore()
    for step in (-1, 1, 2):
        tell(barrier, along(step))
    for d in NEAR:
        tell(barrier, beside(d))
    for xs in range(NX):
        for c in range(2):
            pl.when(jnp.logical_not(home & (core == c) & (xs == x)))(
                functools.partial(tell, barrier, device(x, z, c, xs))
            )
    for d in range(1, NX):
        tell(barrier, (wide, lax.rem(x + d, NX)))

    loads = []
    for n, (src, dst) in enumerate(
        [(feats, halo.at[1, pl.ds(0, ROWS)]), (tok, toks), (koff, offs),
         (w_qkv, wq), (w_out, wo), (w_up, wu), (w_down, wd), (w_tok, wt),
         (w_row, wp.at[:, pl.ds(0, D)]), (w_col, wp.at[:, pl.ds(D, D)])]
    ):
        loads.append(pltpu.make_async_copy(src, dst, wsem.at[n]))
        loads[-1].start()

    for load in loads[:3]:
        load.wait()
    row = lax.broadcasted_iota(jnp.int32, (16, D), 0)
    tok_rel = (toks[...] - 2 * me).astype(f32)
    off4 = jnp.concatenate(
        [offs[...].astype(f32)] + [jnp.zeros((1, 4), f32)] * (D // 4 - 1), axis=1
    )
    meta = jnp.where(row == 0, tok_rel, jnp.where(row == 1, off4, 0.0))
    halo[1, pl.ds(ROWS, 16)] = meta.astype(bf16)
    pl.semaphore_wait(barrier, 3 + 8 + 3 + len(NEAR) - home.astype(jnp.int32))

    sends = [
        pltpu.make_async_remote_copy(
            halo.at[1], halo.at[0], hsend.at[0], hrecv.at[0], along(1), MESH
        ),
        pltpu.make_async_remote_copy(
            halo.at[1], halo.at[2], hsend.at[1], hrecv.at[1], along(-1), MESH
        ),
        pltpu.make_async_remote_copy(
            halo.at[1, pl.ds(0, RIM)], far, hsend.at[2], hrecv.at[2], along(-2), MESH
        ),
    ]
    for s in (sends[2], sends[0], sends[1]):
        s.start()

    for d in NEAR:
        tell(around, beside(d))
    loads[3].wait()
    own = halo[1, pl.ds(0, ROWS)].astype(f32)
    own_proj = project(own, wq[0])
    for load in loads[4:]:
        load.wait()
    pl.semaphore_wait(around, len(NEAR))
    for d in (4, -4):
        tell(beyond.at[0 if d > 0 else 1], beside(d))
    for s in sends:
        s.wait_recv()

    metas = [halo[s, pl.ds(ROWS, 16)].astype(f32) for s in range(3)]
    pieces = [halo[0, pl.ds(0, ROWS)].astype(f32), own]
    pieces += [halo[2, pl.ds(0, ROWS)].astype(f32), far[...].astype(f32)]
    match, counts = matches(metas[1], metas[2])

    near_side = (z > NZ // 2).astype(jnp.int32)

    def pass_on(which):
        pl.semaphore_wait(beyond.at[which], 1)
        tell(rest.at[which], beside(2 - 4 * which))

    state = transform(
        pieces, own_proj, metas, me * ROWS, n_atoms, wq, wo, wu, wd,
        functools.partial(pass_on, near_side),
    )
    atoms = state.astype(bf16)
    means, proj = tokens(atoms, match, counts, wt[...], wp[...])
    mine[0] = proj[0:2, :D]
    mine[1] = proj[0:2, D:]
    slot = lax.rem(wide, 32) * NX + x

    def send_columns(zd, _, part):
        ahead = lax.rem((z - zd) * (1 - 2 * near_side) + NZ, NZ)
        beside_me = (ahead <= 2) | (ahead >= NZ - 2)
        this = (beside_me, (ahead > 2) & (ahead <= 8), (ahead > 8) & (ahead < NZ - 2))[part]

        @pl.when(this)
        def _():
            for dy in (2, 1, 3, 0):
                for dc in (1, 0):
                    to = device(lax.rem(y + dy, NY), zd, lax.rem(core + dc, 2), y)
                    copy = pltpu.make_async_remote_copy(
                        mine.at[1], colbuf.at[slot], csend, crecv, to, MESH
                    )
                    if dy or dc:
                        copy.start()
                    else:
                        pl.when(jnp.logical_not(home & (z == zd)))(copy.start)

        return 0

    def send_part(part):
        lax.fori_loop(0, NZ, functools.partial(send_columns, part=part), 0)

    edge = (z < 4) | (z >= NZ - 4)
    pl.when(edge)(functools.partial(pass_on, 1 - near_side))
    pl.when(z < 4)(functools.partial(send_part, 0))
    pl.semaphore_wait(rest.at[near_side], 1)
    send_part(1)
    pl.when(jnp.logical_not(edge))(functools.partial(pass_on, 1 - near_side))
    pl.when(z >= 4)(functools.partial(send_part, 0))
    pl.semaphore_wait(rest.at[1 - near_side], 1)
    send_part(2)
    pl.when(home)(
        pltpu.make_async_copy(mine.at[1], colbuf.at[slot], crecv).start
    )
    for d in range(1, NX):
        pltpu.make_async_remote_copy(
            mine.at[0], rowbuf.at[x], rsend, rrecv, (wide, lax.rem(x + d, NX)), MESH
        ).start()
    rowbuf[pl.ds(x, 1)] = proj[0:2, :D].reshape(1, 2, D)
    atom_out[...] = atoms[:ROWS]
    single[...] = means[0:2]

    three = rowbuf.at[pl.ds(0, 3)]
    pltpu.make_async_copy(three, three, rrecv).wait()
    for s in range(NX):
        rows_out[pl.ds(2 * s, 2), :] = rowbuf[s].astype(f32)
    pltpu.make_async_copy(colbuf, colbuf, crecv).wait()
    for s in range(128):
        cols_out[pl.ds(2 * s, 2), :] = colbuf[s].astype(f32)
    for s in sends:
        s.wait_send()
    pltpu.make_async_copy(three, three, rsend).wait()
    less = colbuf.at[pl.ds(0, 127)]
    pl.when(home)(pltpu.make_async_copy(less, less, csend).wait)
    pl.when(jnp.logical_not(home))(pltpu.make_async_copy(colbuf, colbuf, csend).wait)


def finish(pair, rows, cols, atoms, means, pair_out, atom_out, single, sums, sem):
    copies = [
        pltpu.make_async_copy(atoms, atom_out, sem.at[0]),
        pltpu.make_async_copy(means, single, sem.at[1]),
    ]
    for copy in copies:
        copy.start()
    cols = cols[...]
    for r in range(8):
        sums[r] = ((pair[r].astype(f32) + rows[pl.ds(r, 1), :]) + cols).astype(bf16)
        copies.append(pltpu.make_async_copy(sums.at[r], pair_out.at[r], sem.at[r + 2]))
        copies[-1].start()
    for copy in copies:
        copy.wait()


def on_device(
    atom_feats, atom_token, key_offset, pair_in, w_qkv, w_out, w_up, w_down, w_tok, w_row, w_col
):
    vmem = pl.BlockSpec(memory_space=pltpu.VMEM)
    hbm = pl.BlockSpec(memory_space=pltpu.HBM)
    dma, flag = pltpu.SemaphoreType.DMA, pltpu.SemaphoreType.REGULAR
    atoms, means, row_vecs, col_vecs = pl.pallas_call(
        functools.partial(kernel, 512 * ROWS),
        out_shape=[
            jax.ShapeDtypeStruct((ROWS, D), bf16),
            jax.ShapeDtypeStruct((2, TOKC), bf16),
            jax.ShapeDtypeStruct((8, D), f32),
            jax.ShapeDtypeStruct((256, D), f32),
        ],
        in_specs=[hbm] * 10,
        out_specs=[vmem] * 4,
        scratch_shapes=[
            pltpu.VMEM((3, ROWS + 16, D), bf16),
            pltpu.VMEM((RIM, D), bf16),
            pltpu.VMEM((1, ROWS), jnp.int32),
            pltpu.VMEM((1, 4), jnp.int32),
            pltpu.VMEM((2, D, 3 * D), bf16),
            pltpu.VMEM((2, D, D), bf16),
            pltpu.VMEM((2, D, 2 * FFH), bf16),
            pltpu.VMEM((2, FFH, D), bf16),
            pltpu.VMEM((D, TOKC), bf16),
            pltpu.VMEM((TOKC, 2 * D), bf16),
            pltpu.VMEM((2, 2, D), bf16),
            pltpu.VMEM((NX, 2, D), bf16),
            pltpu.VMEM((128, 2, D), bf16),
            dma((10,)), dma((3,)), dma((3,)), dma, dma, dma, dma, flag, flag((2,)), flag((2,)),
        ],
        compiler_params=pltpu.CompilerParams(
            collective_id=1, has_side_effects=True, vmem_limit_bytes=32 * 1024 * 1024
        ),
        name="atoms_tokens",
    )(
        *[
            pltpu.with_memory_space_constraint(a, pltpu.HBM)
            for a in (
                atom_feats, atom_token.reshape(1, ROWS), key_offset.reshape(1, 4),
                w_qkv, w_out, w_up, w_down, w_tok, w_row, w_col,
            )
        ]
    )
    pair_out, atom_out, single = pl.pallas_call(
        finish,
        out_shape=[
            jax.ShapeDtypeStruct(pair_in.shape, bf16),
            jax.ShapeDtypeStruct((ROWS, D), bf16),
            jax.ShapeDtypeStruct((2, TOKC), bf16),
        ],
        in_specs=[vmem] * 5,
        out_specs=[hbm] * 3,
        scratch_shapes=[pltpu.VMEM(pair_in.shape, bf16), dma((10,))],
        compiler_params=pltpu.CompilerParams(vmem_limit_bytes=16 * 1024 * 1024),
        name="pair_add",
    )(pair_in, row_vecs, col_vecs, atoms, means)
    return (atom_out, single, pair_out)


def solution(mesh):
    return jax.shard_map(
        on_device,
        mesh=mesh,
        in_specs=(
            P(("wide", "col"), None),
            P(("wide", "col")),
            P(("wide", "col")),
            P("wide", "col", None),
            P(), P(), P(), P(), P(), P(), P(),
        ),
        out_specs=(P(("wide", "col"), None), P(("wide", "col"), None), P("wide", "col", None)),
        check_vma=False,
    )
```

```python
import functools

import jax
import jax.numpy as jnp
from jax import lax
from jax.experimental import pallas as pl
from jax.experimental.pallas import tpu as pltpu
from jax.sharding import PartitionSpec as P

D = 128
HEADS = 4
HEAD = 32
FFH = 256
TOKC = 384
QBLK = 32
KWIN = 128
RIM = 64
ROWS = 128
NY, NZ, NX = 4, 16, 4
NEAR = (2, -2, 1, -1)
SCORE = 1.4426950408889634 / HEAD**0.5
NEG = -1e30
MESH = pl.DeviceIdType.MESH
f32, bf16 = jnp.float32, jnp.bfloat16


def device(y, z, core, x):
    return ((y * NZ + z) * 2 + core, x)


def along(step):
    at = lax.rem(lax.axis_index("wide") * NX + lax.axis_index("col") + step + 512, 512)
    return (at // NX, lax.rem(at, NX))


def dot(a, b):
    return jnp.dot(a, b, preferred_element_type=f32)


def normed_dot(v, w):
    c = v - jnp.mean(v, axis=-1, keepdims=True)
    scale = lax.rsqrt(jnp.mean(c * c, axis=-1, keepdims=True) + 1e-5)
    return dot(c.astype(bf16), w) * scale


def window_bias(offset, block, base, n_key, n_atoms):
    first = base - RIM
    at = base + block * QBLK
    outside = (at < 0) | (at >= n_atoms)
    floor = jnp.where(outside, -KWIN * 8, -first).astype(f32)
    ceil = jnp.where(outside, KWIN * 8, n_atoms - first).astype(f32)
    low = jnp.maximum(offset + float(block * QBLK), floor)
    high = jnp.minimum(offset + float(block * QBLK + KWIN), ceil)
    key = lax.broadcasted_iota(jnp.int32, (1, n_key), 1).astype(f32)
    return jnp.where((key >= low) & (key < high), 0.0, NEG)


def rows_of(blocks, n_key):
    return jnp.concatenate([jnp.broadcast_to(b[:, :n_key], (QBLK, n_key)) for b in blocks], axis=0)


def attend(q, k, v, bias):
    n = q.shape[0]
    lane = lax.broadcasted_iota(jnp.int32, (n, D), 1) // HEAD
    stacked = jnp.concatenate(
        [jnp.where(lane == h, q, jnp.zeros_like(q)) for h in range(HEADS)], axis=0
    )
    scores = lax.dot_general(stacked, k, (((1,), (1,)), ((), ())), preferred_element_type=f32)
    weights = []
    for h in range(HEADS):
        e = jnp.exp2(scores[h * n : (h + 1) * n] * SCORE + bias)
        weights.append((e / jnp.sum(e, axis=-1, keepdims=True)).astype(bf16))
    out = dot(jnp.concatenate(weights, axis=0), v)
    total = jnp.zeros((n, D), f32)
    for h in range(HEADS):
        total = jnp.where(lane == h, out[h * n : (h + 1) * n], total)
    return total.astype(bf16)


def block(state, proj, spans, biases, wo, wu, wd):
    kept = []
    for (row, n), bias in zip(spans, biases):
        lo, hi = row - RIM, row + n + RIM
        kept.append(
            attend(proj[row : row + n, :D], proj[lo:hi, D : 2 * D], proj[lo:hi, 2 * D :], bias)
        )
    first = spans[0][0]
    last = spans[-1][0] + spans[-1][1]
    state = state[first:last] + dot(jnp.concatenate(kept, axis=0), wo)
    hidden = normed_dot(state, wu)
    gate, up = hidden[:, :FFH], hidden[:, FFH:]
    gated = (0.5 * gate * (1.0 + jnp.tanh(0.5 * gate)) * up).astype(bf16)
    return state + dot(gated, wd)


def project(rows, wq):
    return normed_dot(rows, wq).astype(bf16)


def tokens(atoms, match, counts, wt, wp):
    act = jnp.maximum(dot(atoms, wt), 0.0).astype(bf16)
    means = (dot(match, act) / counts).astype(bf16)
    return means, dot(means, wp).astype(bf16)


def matches(own_meta, right_meta):
    rel = jnp.concatenate([own_meta[0:1, :], right_meta[0:1, :RIM] + 2.0], axis=1)
    ids = lax.broadcasted_iota(jnp.int32, (16, ROWS + RIM), 0).astype(f32)
    match = jnp.where(ids == rel, 1.0, 0.0)
    return match.astype(bf16), jnp.maximum(jnp.sum(match, axis=-1, keepdims=True), 1.0)


def biases_of(metas, base, n_atoms):
    out = []
    for start, n, n_key in ((-RIM, RIM, 192), (0, ROWS, 256), (ROWS, ROWS, 256)):
        span = []
        for k in range(n // QBLK):
            at = (start + ROWS) // QBLK + k
            off = metas[at // 4][1:2, at % 4 : at % 4 + 1]
            span.append(window_bias(off, k, base + start, n_key, n_atoms))
        out.append(span)
    return out


SPANS1 = [(64, 64), (128, 128), (256, 128)]
SPANS2 = [(64, 128), (192, 64)]


def transform(pieces, own_proj, metas, base, n_atoms, wq, wo, wu, wd, between):
    left, own, right, far = pieces
    biases = biases_of(metas, base, n_atoms)
    rim = project(jnp.concatenate([left, right, far], axis=0), wq[0])
    proj = jnp.concatenate([rim[:ROWS], own_proj, rim[ROWS:]], axis=0)
    state = jnp.concatenate([left, own, right, far], axis=0)
    bias1 = [rows_of(biases[0], 192), rows_of(biases[1], 256), rows_of(biases[2], 256)]
    state = block(state, proj, SPANS1, bias1, wo[0], wu[0], wd[0])
    between()
    bias2 = [bias1[1], rows_of(biases[2][:2], 192)]
    proj = project(state, wq[1])
    return block(state, proj, SPANS2, bias2, wo[1], wu[1], wd[1])


def kernel(
    n_atoms,
    feats, tok, koff, w_qkv, w_out, w_up, w_down, w_tok, w_row, w_col,
    atom_out, single, rows_out, cols_out,
    halo, far, toks, offs, wq, wo, wu, wd, wt, wp, mine, rowbuf, colbuf,
    wsem, hsend, hrecv, rsend, rrecv, csend, crecv, around, beyond, rest,
):
    wide, x = lax.axis_index("wide"), lax.axis_index("col")
    core = lax.rem(wide, 2)
    z = lax.rem(wide // 2, NZ)
    y = wide // (2 * NZ)
    me = wide * NX + x
    home = x == y

    def tell(sem, dev):
        pl.semaphore_signal(sem, inc=1, device_id=dev, device_id_type=MESH)

    def beside(d):
        return device(y, lax.rem(z + d + NZ, NZ), core, x)

    barrier = pltpu.get_barrier_semaphore()
    for step in (-1, 1, 2):
        tell(barrier, along(step))
    for xs in range(NX):
        for c in range(2):
            pl.when(jnp.logical_not(home & (core == c) & (xs == x)))(
                functools.partial(tell, barrier, device(x, z, c, xs))
            )
    for d in NEAR:
        tell(barrier, beside(d))
    for d in range(1, NX):
        tell(barrier, (wide, lax.rem(x + d, NX)))

    loads = []
    for n, (src, dst) in enumerate(
        [(feats, halo.at[1, pl.ds(0, ROWS)]), (tok, toks), (koff, offs),
         (w_qkv, wq), (w_out, wo), (w_up, wu), (w_down, wd), (w_tok, wt),
         (w_row, wp.at[:, pl.ds(0, D)]), (w_col, wp.at[:, pl.ds(D, D)])]
    ):
        loads.append(pltpu.make_async_copy(src, dst, wsem.at[n]))
        loads[-1].start()

    for load in loads[:3]:
        load.wait()
    row = lax.broadcasted_iota(jnp.int32, (16, D), 0)
    tok_rel = (toks[...] - 2 * me).astype(f32)
    off4 = jnp.concatenate(
        [offs[...].astype(f32)] + [jnp.zeros((1, 4), f32)] * (D // 4 - 1), axis=1
    )
    meta = jnp.where(row == 0, tok_rel, jnp.where(row == 1, off4, 0.0))
    halo[1, pl.ds(ROWS, 16)] = meta.astype(bf16)
    pl.semaphore_wait(barrier, 3 + 8 + 3 + len(NEAR) - home.astype(jnp.int32))

    sends = [
        pltpu.make_async_remote_copy(
            halo.at[1], halo.at[0], hsend.at[0], hrecv.at[0], along(1), MESH
        ),
        pltpu.make_async_remote_copy(
            halo.at[1], halo.at[2], hsend.at[1], hrecv.at[1], along(-1), MESH
        ),
        pltpu.make_async_remote_copy(
            halo.at[1, pl.ds(0, RIM)], far, hsend.at[2], hrecv.at[2], along(-2), MESH
        ),
    ]
    for s in (sends[2], sends[0], sends[1]):
        s.start()

    for d in NEAR:
        tell(around, beside(d))
    loads[3].wait()
    own = halo[1, pl.ds(0, ROWS)].astype(f32)
    own_proj = project(own, wq[0])
    for load in loads[4:]:
        load.wait()
    pl.semaphore_wait(around, len(NEAR))
    for d in (4, -4):
        tell(beyond.at[0 if d > 0 else 1], beside(d))
    for s in sends:
        s.wait_recv()

    metas = [halo[s, pl.ds(ROWS, 16)].astype(f32) for s in range(3)]
    ends = n_atoms // ROWS
    left = jnp.where(me == 0, 0.0, halo[0, pl.ds(0, ROWS)].astype(f32))
    right = jnp.where(me == ends - 1, 0.0, halo[2, pl.ds(0, ROWS)].astype(f32))
    pieces = [left, own, right, jnp.where(me >= ends - 2, 0.0, far[...].astype(f32))]
    match, counts = matches(metas[1], metas[2])

    near_side = (z > NZ // 2).astype(jnp.int32)

    def pass_on(which):
        pl.semaphore_wait(beyond.at[which], 1)
        tell(rest.at[which], beside(2 - 4 * which))

    state = transform(
        pieces, own_proj, metas, me * ROWS, n_atoms, wq, wo, wu, wd,
        functools.partial(pass_on, near_side),
    )
    atoms = state.astype(bf16)
    means, proj = tokens(atoms, match, counts, wt[...], wp[...])
    mine[0] = proj[0:2, :D]
    mine[1] = proj[0:2, D:]
    slot = lax.rem(wide, 32) * NX + x

    def send_columns(zd, _, part):
        ahead = lax.rem((z - zd) * (1 - 2 * near_side) + NZ, NZ)
        beside_me = (ahead <= 2) | (ahead >= NZ - 2)
        this = (beside_me, (ahead > 2) & (ahead <= 8), (ahead > 8) & (ahead < NZ - 2))[part]

        @pl.when(this)
        def _():
            for dy in (2, 1, 3, 0):
                for dc in (1, 0):
                    to = device(lax.rem(y + dy, NY), zd, lax.rem(core + dc, 2), y)
                    copy = pltpu.make_async_remote_copy(
                        mine.at[1], colbuf.at[slot], csend, crecv, to, MESH
                    )
                    if dy or dc:
                        copy.start()
                    else:
                        pl.when(jnp.logical_not(home & (z == zd)))(copy.start)

        return 0

    def send_part(part):
        lax.fori_loop(0, NZ, functools.partial(send_columns, part=part), 0)

    edge = (z < 4) | (z >= NZ - 4)
    pl.when(edge)(functools.partial(pass_on, 1 - near_side))
    pl.when(z < 4)(functools.partial(send_part, 0))
    pl.semaphore_wait(rest.at[near_side], 1)
    send_part(1)
    pl.when(jnp.logical_not(edge))(functools.partial(pass_on, 1 - near_side))
    pl.when(z >= 4)(functools.partial(send_part, 0))
    pl.semaphore_wait(rest.at[1 - near_side], 1)
    send_part(2)
    pl.when(home)(
        pltpu.make_async_copy(mine.at[1], colbuf.at[slot], crecv).start
    )
    for d in range(1, NX):
        pltpu.make_async_remote_copy(
            mine.at[0], rowbuf.at[x], rsend, rrecv, (wide, lax.rem(x + d, NX)), MESH
        ).start()
    rowbuf[pl.ds(x, 1)] = proj[0:2, :D].reshape(1, 2, D)
    atom_out[...] = atoms[:ROWS]
    single[...] = means[0:2]

    three = rowbuf.at[pl.ds(0, 3)]
    pltpu.make_async_copy(three, three, rrecv).wait()
    for s in range(NX):
        rows_out[pl.ds(2 * s, 2), :] = rowbuf[s].astype(f32)
    pltpu.make_async_copy(colbuf, colbuf, crecv).wait()
    for s in range(128):
        cols_out[pl.ds(2 * s, 2), :] = colbuf[s].astype(f32)
    for s in sends:
        s.wait_send()
    pltpu.make_async_copy(three, three, rsend).wait()
    less = colbuf.at[pl.ds(0, 127)]
    pl.when(home)(pltpu.make_async_copy(less, less, csend).wait)
    pl.when(jnp.logical_not(home))(pltpu.make_async_copy(colbuf, colbuf, csend).wait)


def finish(pair, rows, cols, atoms, means, pair_out, atom_out, single, sums, sem):
    copies = [
        pltpu.make_async_copy(atoms, atom_out, sem.at[0]),
        pltpu.make_async_copy(means, single, sem.at[1]),
    ]
    for copy in copies:
        copy.start()
    cols = cols[...]
    for r in range(8):
        sums[r] = ((pair[r].astype(f32) + rows[pl.ds(r, 1), :]) + cols).astype(bf16)
        copies.append(pltpu.make_async_copy(sums.at[r], pair_out.at[r], sem.at[r + 2]))
        copies[-1].start()
    for copy in copies:
        copy.wait()


def on_device(
    atom_feats, atom_token, key_offset, pair_in, w_qkv, w_out, w_up, w_down, w_tok, w_row, w_col
):
    vmem = pl.BlockSpec(memory_space=pltpu.VMEM)
    hbm = pl.BlockSpec(memory_space=pltpu.HBM)
    dma, flag = pltpu.SemaphoreType.DMA, pltpu.SemaphoreType.REGULAR
    atoms, means, row_vecs, col_vecs = pl.pallas_call(
        functools.partial(kernel, 512 * ROWS),
        out_shape=[
            jax.ShapeDtypeStruct((ROWS, D), bf16),
            jax.ShapeDtypeStruct((2, TOKC), bf16),
            jax.ShapeDtypeStruct((8, D), f32),
            jax.ShapeDtypeStruct((256, D), f32),
        ],
        in_specs=[hbm] * 10,
        out_specs=[vmem] * 4,
        scratch_shapes=[
            pltpu.VMEM((3, ROWS + 16, D), bf16),
            pltpu.VMEM((RIM, D), bf16),
            pltpu.VMEM((1, ROWS), jnp.int32),
            pltpu.VMEM((1, 4), jnp.int32),
            pltpu.VMEM((2, D, 3 * D), bf16),
            pltpu.VMEM((2, D, D), bf16),
            pltpu.VMEM((2, D, 2 * FFH), bf16),
            pltpu.VMEM((2, FFH, D), bf16),
            pltpu.VMEM((D, TOKC), bf16),
            pltpu.VMEM((TOKC, 2 * D), bf16),
            pltpu.VMEM((2, 2, D), bf16),
            pltpu.VMEM((NX, 2, D), bf16),
            pltpu.VMEM((128, 2, D), bf16),
            dma((10,)), dma((3,)), dma((3,)), dma, dma, dma, dma, flag, flag((2,)), flag((2,)),
        ],
        compiler_params=pltpu.CompilerParams(
            collective_id=1, has_side_effects=True, vmem_limit_bytes=32 * 1024 * 1024
        ),
        name="atoms_tokens",
    )(
        *[
            pltpu.with_memory_space_constraint(a, pltpu.HBM)
            for a in (
                atom_feats, atom_token.reshape(1, ROWS), key_offset.reshape(1, 4),
                w_qkv, w_out, w_up, w_down, w_tok, w_row, w_col,
            )
        ]
    )
    pair_out, atom_out, single = pl.pallas_call(
        finish,
        out_shape=[
            jax.ShapeDtypeStruct(pair_in.shape, bf16),
            jax.ShapeDtypeStruct((ROWS, D), bf16),
            jax.ShapeDtypeStruct((2, TOKC), bf16),
        ],
        in_specs=[vmem] * 5,
        out_specs=[hbm] * 3,
        scratch_shapes=[pltpu.VMEM(pair_in.shape, bf16), dma((10,))],
        compiler_params=pltpu.CompilerParams(vmem_limit_bytes=16 * 1024 * 1024),
        name="pair_add",
    )(pair_in, row_vecs, col_vecs, atoms, means)
    return (atom_out, single, pair_out)


def solution(mesh):
    return jax.shard_map(
        on_device,
        mesh=mesh,
        in_specs=(
            P(("wide", "col"), None),
            P(("wide", "col")),
            P(("wide", "col")),
            P("wide", "col", None),
            P(), P(), P(), P(), P(), P(), P(),
        ),
        out_specs=(P(("wide", "col"), None), P(("wide", "col"), None), P("wide", "col", None)),
        check_vma=False,
    )
```

```python
import functools

import jax
import jax.numpy as jnp
from jax import lax
from jax.experimental import pallas as pl
from jax.experimental.pallas import tpu as pltpu
from jax.sharding import PartitionSpec as P

D = 128
HEADS = 4
HEAD = 32
FFH = 256
TOKC = 384
QBLK = 32
KWIN = 128
RIM = 64
ROWS = 128
NY, NZ, NX = 4, 16, 4
NEAR = (2, -2, 1, -1)
SCORE = 1.4426950408889634 / HEAD**0.5
NEG = -1e30
MESH = pl.DeviceIdType.MESH
f32, bf16 = jnp.float32, jnp.bfloat16


def device(y, z, core, x):
    return ((y * NZ + z) * 2 + core, x)


def along(step):
    at = lax.rem(lax.axis_index("wide") * NX + lax.axis_index("col") + step + 512, 512)
    return (at // NX, lax.rem(at, NX))


def dot(a, b):
    return jnp.dot(a, b, preferred_element_type=f32)


def normed_dot(v, w):
    c = v - jnp.mean(v, axis=-1, keepdims=True)
    scale = lax.rsqrt(jnp.mean(c * c, axis=-1, keepdims=True) + 1e-5)
    return dot(c.astype(bf16), w) * scale


def window_bias(offset, block, base, n_key, n_atoms):
    first = base - RIM
    at = base + block * QBLK
    outside = (at < 0) | (at >= n_atoms)
    floor = jnp.where(outside, -KWIN * 8, -first).astype(f32)
    ceil = jnp.where(outside, KWIN * 8, n_atoms - first).astype(f32)
    low = jnp.maximum(offset + float(block * QBLK), floor)
    high = jnp.minimum(offset + float(block * QBLK + KWIN), ceil)
    key = lax.broadcasted_iota(jnp.int32, (1, n_key), 1).astype(f32)
    return jnp.where((key >= low) & (key < high), 0.0, NEG)


def rows_of(blocks, n_key):
    return jnp.concatenate([jnp.broadcast_to(b[:, :n_key], (QBLK, n_key)) for b in blocks], axis=0)


def attend(q, k, v, bias):
    n = q.shape[0]
    lane = lax.broadcasted_iota(jnp.int32, (n, D), 1) // HEAD
    stacked = jnp.concatenate(
        [jnp.where(lane == h, q, jnp.zeros_like(q)) for h in range(HEADS)], axis=0
    )
    scores = lax.dot_general(stacked, k, (((1,), (1,)), ((), ())), preferred_element_type=f32)
    weights = []
    for h in range(HEADS):
        e = jnp.exp2(scores[h * n : (h + 1) * n] * SCORE + bias)
        weights.append((e / jnp.sum(e, axis=-1, keepdims=True)).astype(bf16))
    out = dot(jnp.concatenate(weights, axis=0), v)
    total = jnp.zeros((n, D), f32)
    for h in range(HEADS):
        total = jnp.where(lane == h, out[h * n : (h + 1) * n], total)
    return total.astype(bf16)


def block(state, proj, spans, biases, wo, wu, wd):
    kept = []
    for (row, n), bias in zip(spans, biases):
        lo, hi = row - RIM, row + n + RIM
        kept.append(
            attend(proj[row : row + n, :D], proj[lo:hi, D : 2 * D], proj[lo:hi, 2 * D :], bias)
        )
    first = spans[0][0]
    last = spans[-1][0] + spans[-1][1]
    state = state[first:last] + dot(jnp.concatenate(kept, axis=0), wo)
    hidden = normed_dot(state, wu)
    gate, up = hidden[:, :FFH], hidden[:, FFH:]
    gated = (0.5 * gate * (1.0 + jnp.tanh(0.5 * gate)) * up).astype(bf16)
    return state + dot(gated, wd)


def project(rows, wq):
    return normed_dot(rows, wq).astype(bf16)


def tokens(atoms, match, counts, wt, wp):
    act = jnp.maximum(dot(atoms, wt), 0.0).astype(bf16)
    means = (dot(match, act) / counts).astype(bf16)
    return means, dot(means, wp).astype(bf16)


def matches(own_meta, right_meta):
    rel = jnp.concatenate([own_meta[0:1, :], right_meta[0:1, :RIM] + 2.0], axis=1)
    ids = lax.broadcasted_iota(jnp.int32, (16, ROWS + RIM), 0).astype(f32)
    match = jnp.where(ids == rel, 1.0, 0.0)
    return match.astype(bf16), jnp.maximum(jnp.sum(match, axis=-1, keepdims=True), 1.0)


def biases_of(metas, base, n_atoms):
    out = []
    for start, n, n_key in ((-RIM, RIM, 192), (0, ROWS, 256), (ROWS, ROWS, 256)):
        span = []
        for k in range(n // QBLK):
            at = (start + ROWS) // QBLK + k
            off = metas[at // 4][1:2, at % 4 : at % 4 + 1]
            span.append(window_bias(off, k, base + start, n_key, n_atoms))
        out.append(span)
    return out


SPANS1 = [(64, 64), (128, 128), (256, 128)]
SPANS2 = [(64, 128), (192, 64)]


def transform(pieces, own_proj, metas, base, n_atoms, wq, wo, wu, wd, between):
    left, own, right, far = pieces
    biases = biases_of(metas, base, n_atoms)
    rim = project(jnp.concatenate([left, right, far], axis=0), wq[0])
    proj = jnp.concatenate([rim[:ROWS], own_proj, rim[ROWS:]], axis=0)
    state = jnp.concatenate([left, own, right, far], axis=0)
    bias1 = [rows_of(biases[0], 192), rows_of(biases[1], 256), rows_of(biases[2], 256)]
    state = block(state, proj, SPANS1, bias1, wo[0], wu[0], wd[0])
    between()
    bias2 = [bias1[1], rows_of(biases[2][:2], 192)]
    proj = project(state, wq[1])
    return block(state, proj, SPANS2, bias2, wo[1], wu[1], wd[1])


def kernel(
    n_atoms,
    feats, tok, koff, w_qkv, w_out, w_up, w_down, w_tok, w_row, w_col,
    atom_out, single, rows_out, cols_out,
    halo, far, toks, offs, wq, wo, wu, wd, wt, wp, mine, rowbuf, colbuf,
    wsem, hsend, hrecv, rsend, rrecv, csend, crecv, around, beyond, rest,
):
    wide, x = lax.axis_index("wide"), lax.axis_index("col")
    core = lax.rem(wide, 2)
    z = lax.rem(wide // 2, NZ)
    y = wide // (2 * NZ)
    me = wide * NX + x
    home = x == y

    def tell(sem, dev):
        pl.semaphore_signal(sem, inc=1, device_id=dev, device_id_type=MESH)

    def beside(d):
        return device(y, lax.rem(z + d + NZ, NZ), core, x)

    barrier = pltpu.get_barrier_semaphore()
    for step in (-1, 1, 2):
        tell(barrier, along(step))
    for d in NEAR:
        tell(barrier, beside(d))
    for xs in range(NX):
        for c in range(2):
            pl.when(jnp.logical_not(home & (core == c) & (xs == x)))(
                functools.partial(tell, barrier, device(x, z, c, xs))
            )
    for d in range(1, NX):
        tell(barrier, (wide, lax.rem(x + d, NX)))

    loads = []
    for n, (src, dst) in enumerate(
        [(feats, halo.at[1, pl.ds(0, ROWS)]), (tok, toks), (koff, offs),
         (w_qkv, wq), (w_out, wo), (w_up, wu), (w_down, wd), (w_tok, wt),
         (w_row, wp.at[:, pl.ds(0, D)]), (w_col, wp.at[:, pl.ds(D, D)])]
    ):
        loads.append(pltpu.make_async_copy(src, dst, wsem.at[n]))
        loads[-1].start()

    for load in loads[:3]:
        load.wait()
    row = lax.broadcasted_iota(jnp.int32, (16, D), 0)
    tok_rel = (toks[...] - 2 * me).astype(f32)
    off4 = jnp.concatenate(
        [offs[...].astype(f32)] + [jnp.zeros((1, 4), f32)] * (D // 4 - 1), axis=1
    )
    meta = jnp.where(row == 0, tok_rel, jnp.where(row == 1, off4, 0.0))
    halo[1, pl.ds(ROWS, 16)] = meta.astype(bf16)
    pl.semaphore_wait(barrier, 3 + 8 + 3 + len(NEAR) - home.astype(jnp.int32))

    sends = [
        pltpu.make_async_remote_copy(
            halo.at[1], halo.at[0], hsend.at[0], hrecv.at[0], along(1), MESH
        ),
        pltpu.make_async_remote_copy(
            halo.at[1], halo.at[2], hsend.at[1], hrecv.at[1], along(-1), MESH
        ),
        pltpu.make_async_remote_copy(
            halo.at[1, pl.ds(0, RIM)], far, hsend.at[2], hrecv.at[2], along(-2), MESH
        ),
    ]
    for s in (sends[2], sends[0], sends[1]):
        s.start()

    for d in NEAR:
        tell(around, beside(d))
    loads[3].wait()
    own = halo[1, pl.ds(0, ROWS)].astype(f32)
    own_proj = project(own, wq[0])
    for load in loads[4:]:
        load.wait()
    pl.semaphore_wait(around, len(NEAR))
    for d in (4, -4):
        tell(beyond.at[0 if d > 0 else 1], beside(d))
    for s in sends:
        s.wait_recv()

    metas = [halo[s, pl.ds(ROWS, 16)].astype(f32) for s in range(3)]
    ends = n_atoms // ROWS
    left = jnp.where(me == 0, 0.0, halo[0, pl.ds(0, ROWS)].astype(f32))
    right = jnp.where(me == ends - 1, 0.0, halo[2, pl.ds(0, ROWS)].astype(f32))
    pieces = [left, own, right, jnp.where(me >= ends - 2, 0.0, far[...].astype(f32))]
    match, counts = matches(metas[1], metas[2])

    near_side = (z > NZ // 2).astype(jnp.int32)

    def pass_on(which):
        pl.semaphore_wait(beyond.at[which], 1)
        tell(rest.at[which], beside(2 - 4 * which))

    state = transform(
        pieces, own_proj, metas, me * ROWS, n_atoms, wq, wo, wu, wd,
        functools.partial(pass_on, near_side),
    )
    atoms = state.astype(bf16)
    means, proj = tokens(atoms, match, counts, wt[...], wp[...])
    mine[0] = proj[0:2, :D]
    mine[1] = proj[0:2, D:]
    slot = lax.rem(wide, 32) * NX + x

    def send_columns(zd, _, part):
        ahead = lax.rem((z - zd) * (1 - 2 * near_side) + NZ, NZ)
        beside_me = (ahead <= 2) | (ahead >= NZ - 2)
        this = (beside_me, (ahead > 2) & (ahead <= 8), (ahead > 8) & (ahead < NZ - 2))[part]

        @pl.when(this)
        def _():
            for dy in (2, 1, 3, 0):
                for dc in (1, 0):
                    to = device(lax.rem(y + dy, NY), zd, lax.rem(core + dc, 2), y)
                    copy = pltpu.make_async_remote_copy(
                        mine.at[1], colbuf.at[slot], csend, crecv, to, MESH
                    )
                    if dy or dc:
                        copy.start()
                    else:
                        pl.when(jnp.logical_not(home & (z == zd)))(copy.start)

        return 0

    def send_part(part):
        lax.fori_loop(0, NZ, functools.partial(send_columns, part=part), 0)

    edge = (z < 4) | (z >= NZ - 4)
    pl.when(edge)(functools.partial(pass_on, 1 - near_side))
    pl.when(z < 4)(functools.partial(send_part, 0))
    pl.semaphore_wait(rest.at[near_side], 1)
    send_part(1)
    pl.when(jnp.logical_not(edge))(functools.partial(pass_on, 1 - near_side))
    pl.when(z >= 4)(functools.partial(send_part, 0))
    pl.semaphore_wait(rest.at[1 - near_side], 1)
    send_part(2)
    pl.when(home)(
        pltpu.make_async_copy(mine.at[1], colbuf.at[slot], crecv).start
    )
    for d in range(1, NX):
        pltpu.make_async_remote_copy(
            mine.at[0], rowbuf.at[x], rsend, rrecv, (wide, lax.rem(x + d, NX)), MESH
        ).start()
    rowbuf[pl.ds(x, 1)] = proj[0:2, :D].reshape(1, 2, D)
    atom_out[...] = atoms[:ROWS]
    single[...] = means[0:2]

    three = rowbuf.at[pl.ds(0, 3)]
    pltpu.make_async_copy(three, three, rrecv).wait()
    for s in range(NX):
        rows_out[pl.ds(2 * s, 2), :] = rowbuf[s].astype(f32)
    pltpu.make_async_copy(colbuf, colbuf, crecv).wait()
    for s in range(128):
        cols_out[pl.ds(2 * s, 2), :] = colbuf[s].astype(f32)
    for s in sends:
        s.wait_send()
    pltpu.make_async_copy(three, three, rsend).wait()
    less = colbuf.at[pl.ds(0, 127)]
    pl.when(home)(pltpu.make_async_copy(less, less, csend).wait)
    pl.when(jnp.logical_not(home))(pltpu.make_async_copy(colbuf, colbuf, csend).wait)


def finish(pair, rows, cols, atoms, means, pair_out, atom_out, single, sums, sem):
    copies = [
        pltpu.make_async_copy(atoms, atom_out, sem.at[0]),
        pltpu.make_async_copy(means, single, sem.at[1]),
    ]
    for copy in copies:
        copy.start()
    cols = cols[...]
    for r in range(8):
        sums[r] = ((pair[r].astype(f32) + rows[pl.ds(r, 1), :]) + cols).astype(bf16)
        copies.append(pltpu.make_async_copy(sums.at[r], pair_out.at[r], sem.at[r + 2]))
        copies[-1].start()
    for copy in copies:
        copy.wait()


def on_device(
    atom_feats, atom_token, key_offset, pair_in, w_qkv, w_out, w_up, w_down, w_tok, w_row, w_col
):
    vmem = pl.BlockSpec(memory_space=pltpu.VMEM)
    hbm = pl.BlockSpec(memory_space=pltpu.HBM)
    dma, flag = pltpu.SemaphoreType.DMA, pltpu.SemaphoreType.REGULAR
    atoms, means, row_vecs, col_vecs = pl.pallas_call(
        functools.partial(kernel, 512 * ROWS),
        out_shape=[
            jax.ShapeDtypeStruct((ROWS, D), bf16),
            jax.ShapeDtypeStruct((2, TOKC), bf16),
            jax.ShapeDtypeStruct((8, D), f32),
            jax.ShapeDtypeStruct((256, D), f32),
        ],
        in_specs=[hbm] * 10,
        out_specs=[vmem] * 4,
        scratch_shapes=[
            pltpu.VMEM((3, ROWS + 16, D), bf16),
            pltpu.VMEM((RIM, D), bf16),
            pltpu.VMEM((1, ROWS), jnp.int32),
            pltpu.VMEM((1, 4), jnp.int32),
            pltpu.VMEM((2, D, 3 * D), bf16),
            pltpu.VMEM((2, D, D), bf16),
            pltpu.VMEM((2, D, 2 * FFH), bf16),
            pltpu.VMEM((2, FFH, D), bf16),
            pltpu.VMEM((D, TOKC), bf16),
            pltpu.VMEM((TOKC, 2 * D), bf16),
            pltpu.VMEM((2, 2, D), bf16),
            pltpu.VMEM((NX, 2, D), bf16),
            pltpu.VMEM((128, 2, D), bf16),
            dma((10,)), dma((3,)), dma((3,)), dma, dma, dma, dma, flag, flag((2,)), flag((2,)),
        ],
        compiler_params=pltpu.CompilerParams(
            collective_id=1, has_side_effects=True, vmem_limit_bytes=32 * 1024 * 1024
        ),
        name="atoms_tokens",
    )(
        *[
            pltpu.with_memory_space_constraint(a, pltpu.HBM)
            for a in (
                atom_feats, atom_token.reshape(1, ROWS), key_offset.reshape(1, 4),
                w_qkv, w_out, w_up, w_down, w_tok, w_row, w_col,
            )
        ]
    )
    pair_out, atom_out, single = pl.pallas_call(
        finish,
        out_shape=[
            jax.ShapeDtypeStruct(pair_in.shape, bf16),
            jax.ShapeDtypeStruct((ROWS, D), bf16),
            jax.ShapeDtypeStruct((2, TOKC), bf16),
        ],
        in_specs=[vmem] * 5,
        out_specs=[hbm] * 3,
        scratch_shapes=[pltpu.VMEM(pair_in.shape, bf16), dma((10,))],
        compiler_params=pltpu.CompilerParams(vmem_limit_bytes=16 * 1024 * 1024),
        name="pair_add",
    )(pair_in, row_vecs, col_vecs, atoms, means)
    return (atom_out, single, pair_out)


def solution(mesh):
    return jax.shard_map(
        on_device,
        mesh=mesh,
        in_specs=(
            P(("wide", "col"), None),
            P(("wide", "col")),
            P(("wide", "col")),
            P("wide", "col", None),
            P(), P(), P(), P(), P(), P(), P(),
        ),
        out_specs=(P(("wide", "col"), None), P(("wide", "col"), None), P("wide", "col", None)),
        check_vma=False,
    )
```

```python
import functools

import jax
import jax.numpy as jnp
from jax import lax
from jax.experimental import pallas as pl
from jax.experimental.pallas import tpu as pltpu
from jax.sharding import PartitionSpec as P

D = 128
HEADS = 4
HEAD = 32
FFH = 256
TOKC = 384
QBLK = 32
KWIN = 128
RIM = 64
ROWS = 128
NY, NZ, NX = 4, 16, 4
NEAR = (2, -2, 1, -1)
SCORE = 1.4426950408889634 / HEAD**0.5
NEG = -1e30
MESH = pl.DeviceIdType.MESH
f32, bf16 = jnp.float32, jnp.bfloat16


def device(y, z, core, x):
    return ((y * NZ + z) * 2 + core, x)


def along(step):
    at = lax.rem(lax.axis_index("wide") * NX + lax.axis_index("col") + step + 512, 512)
    return (at // NX, lax.rem(at, NX))


def dot(a, b):
    return jnp.dot(a, b, preferred_element_type=f32)


def normed_dot(v, w):
    c = v - jnp.mean(v, axis=-1, keepdims=True)
    scale = lax.rsqrt(jnp.mean(c * c, axis=-1, keepdims=True) + 1e-5)
    return dot(c.astype(bf16), w) * scale


def window_bias(offset, block, base, n_key, n_atoms):
    first = base - RIM
    at = base + block * QBLK
    outside = (at < 0) | (at >= n_atoms)
    floor = jnp.where(outside, -KWIN * 8, -first).astype(f32)
    ceil = jnp.where(outside, KWIN * 8, n_atoms - first).astype(f32)
    low = jnp.maximum(offset + float(block * QBLK), floor)
    high = jnp.minimum(offset + float(block * QBLK + KWIN), ceil)
    key = lax.broadcasted_iota(jnp.int32, (1, n_key), 1).astype(f32)
    return jnp.where((key >= low) & (key < high), 0.0, NEG)


def rows_of(blocks, n_key):
    return jnp.concatenate([jnp.broadcast_to(b[:, :n_key], (QBLK, n_key)) for b in blocks], axis=0)


def attend(q, k, v, bias):
    n = q.shape[0]
    lane = lax.broadcasted_iota(jnp.int32, (n, D), 1) // HEAD
    stacked = jnp.concatenate(
        [jnp.where(lane == h, q, jnp.zeros_like(q)) for h in range(HEADS)], axis=0
    )
    scores = lax.dot_general(stacked, k, (((1,), (1,)), ((), ())), preferred_element_type=f32)
    weights = []
    for h in range(HEADS):
        e = jnp.exp2(scores[h * n : (h + 1) * n] * SCORE + bias)
        weights.append((e / jnp.sum(e, axis=-1, keepdims=True)).astype(bf16))
    out = dot(jnp.concatenate(weights, axis=0), v)
    total = jnp.zeros((n, D), f32)
    for h in range(HEADS):
        total = jnp.where(lane == h, out[h * n : (h + 1) * n], total)
    return total.astype(bf16)


def block(state, proj, spans, biases, wo, wu, wd):
    kept = []
    for (row, n), bias in zip(spans, biases):
        lo, hi = row - RIM, row + n + RIM
        kept.append(
            attend(proj[row : row + n, :D], proj[lo:hi, D : 2 * D], proj[lo:hi, 2 * D :], bias)
        )
    first = spans[0][0]
    last = spans[-1][0] + spans[-1][1]
    state = state[first:last] + dot(jnp.concatenate(kept, axis=0), wo)
    hidden = normed_dot(state, wu)
    gate, up = hidden[:, :FFH], hidden[:, FFH:]
    gated = (0.5 * gate * (1.0 + jnp.tanh(0.5 * gate)) * up).astype(bf16)
    return state + dot(gated, wd)


def project(rows, wq):
    return normed_dot(rows, wq).astype(bf16)


def tokens(atoms, match, counts, wt, wp):
    act = jnp.maximum(dot(atoms, wt), 0.0).astype(bf16)
    means = (dot(match, act) / counts).astype(bf16)
    return means, dot(means, wp).astype(bf16)


def matches(own_meta, right_meta):
    rel = jnp.concatenate([own_meta[0:1, :], right_meta[0:1, :RIM] + 2.0], axis=1)
    ids = lax.broadcasted_iota(jnp.int32, (16, ROWS + RIM), 0).astype(f32)
    match = jnp.where(ids == rel, 1.0, 0.0)
    return match.astype(bf16), jnp.maximum(jnp.sum(match, axis=-1, keepdims=True), 1.0)


def biases_of(metas, base, n_atoms):
    out = []
    for start, n, n_key in ((-RIM, RIM, 192), (0, ROWS, 256), (ROWS, ROWS, 256)):
        span = []
        for k in range(n // QBLK):
            at = (start + ROWS) // QBLK + k
            off = metas[at // 4][1:2, at % 4 : at % 4 + 1]
            span.append(window_bias(off, k, base + start, n_key, n_atoms))
        out.append(span)
    return out


SPANS1 = [(64, 64), (128, 128), (256, 128)]
SPANS2 = [(64, 128), (192, 64)]


def transform(pieces, rim, own_proj, metas, base, n_atoms, wq, wo, wu, wd, between):
    left, own, right, far = pieces
    biases = biases_of(metas, base, n_atoms)
    proj = jnp.concatenate([rim[:ROWS], own_proj, rim[ROWS:]], axis=0)
    state = jnp.concatenate([left, own, right, far], axis=0)
    bias1 = [rows_of(biases[0], 192), rows_of(biases[1], 256), rows_of(biases[2], 256)]
    state = block(state, proj, SPANS1, bias1, wo[0], wu[0], wd[0])
    between()
    bias2 = [bias1[1], rows_of(biases[2][:2], 192)]
    proj = project(state, wq[1])
    return block(state, proj, SPANS2, bias2, wo[1], wu[1], wd[1])


def kernel(
    n_atoms,
    feats, tok, koff, w_qkv, w_out, w_up, w_down, w_tok, w_row, w_col,
    atom_out, single, rows_out, cols_out,
    halo, far, toks, offs, wq, wo, wu, wd, wt, wp, mine, rowbuf, colbuf,
    wsem, hsend, hrecv, rsend, rrecv, csend, crecv, around, beyond, rest,
):
    wide, x = lax.axis_index("wide"), lax.axis_index("col")
    core = lax.rem(wide, 2)
    z = lax.rem(wide // 2, NZ)
    y = wide // (2 * NZ)
    me = wide * NX + x
    home = x == y

    def tell(sem, dev):
        pl.semaphore_signal(sem, inc=1, device_id=dev, device_id_type=MESH)

    def beside(d):
        return device(y, lax.rem(z + d + NZ, NZ), core, x)

    barrier = pltpu.get_barrier_semaphore()
    for step in (-1, 1, 2):
        tell(barrier, along(step))
    for d in NEAR:
        tell(barrier, beside(d))
    for xs in range(NX):
        for c in range(2):
            pl.when(jnp.logical_not(home & (core == c) & (xs == x)))(
                functools.partial(tell, barrier, device(x, z, c, xs))
            )
    for d in range(1, NX):
        tell(barrier, (wide, lax.rem(x + d, NX)))

    loads = []
    for n, (src, dst) in enumerate(
        [(feats, halo.at[1, pl.ds(0, ROWS)]), (tok, toks), (koff, offs),
         (w_qkv, wq), (w_out, wo), (w_up, wu), (w_down, wd), (w_tok, wt),
         (w_row, wp.at[:, pl.ds(0, D)]), (w_col, wp.at[:, pl.ds(D, D)])]
    ):
        loads.append(pltpu.make_async_copy(src, dst, wsem.at[n]))
        loads[-1].start()

    for load in loads[:3]:
        load.wait()
    row = lax.broadcasted_iota(jnp.int32, (16, D), 0)
    tok_rel = (toks[...] - 2 * me).astype(f32)
    off4 = jnp.concatenate(
        [offs[...].astype(f32)] + [jnp.zeros((1, 4), f32)] * (D // 4 - 1), axis=1
    )
    meta = jnp.where(row == 0, tok_rel, jnp.where(row == 1, off4, 0.0))
    halo[1, pl.ds(ROWS, 16)] = meta.astype(bf16)
    pl.semaphore_wait(barrier, 3 + 8 + 3 + len(NEAR) - home.astype(jnp.int32))

    sends = [
        pltpu.make_async_remote_copy(
            halo.at[1], halo.at[0], hsend.at[0], hrecv.at[0], along(1), MESH
        ),
        pltpu.make_async_remote_copy(
            halo.at[1], halo.at[2], hsend.at[1], hrecv.at[1], along(-1), MESH
        ),
        pltpu.make_async_remote_copy(
            halo.at[1, pl.ds(0, RIM)], far, hsend.at[2], hrecv.at[2], along(-2), MESH
        ),
    ]
    for s in (sends[2], sends[0], sends[1]):
        s.start()

    for d in NEAR:
        tell(around, beside(d))
    loads[3].wait()
    own = halo[1, pl.ds(0, ROWS)].astype(f32)
    own_proj = project(own, wq[0])
    for load in loads[4:]:
        load.wait()
    pl.semaphore_wait(around, len(NEAR))
    for d in (4, -4):
        tell(beyond.at[0 if d > 0 else 1], beside(d))
    for s in sends[:2]:
        s.wait_recv()

    metas = [halo[s, pl.ds(ROWS, 16)].astype(f32) for s in range(3)]
    ends = n_atoms // ROWS
    left = jnp.where(me == 0, 0.0, halo[0, pl.ds(0, ROWS)].astype(f32))
    right = jnp.where(me == ends - 1, 0.0, halo[2, pl.ds(0, ROWS)].astype(f32))
    rim = project(jnp.concatenate([left, right], axis=0), wq[0])
    sends[2].wait_recv()
    pieces = [left, own, right, jnp.where(me >= ends - 2, 0.0, far[...].astype(f32))]
    rim = jnp.concatenate([rim, project(pieces[3], wq[0])], axis=0)
    match, counts = matches(metas[1], metas[2])

    near_side = (z > NZ // 2).astype(jnp.int32)

    def pass_on(which):
        pl.semaphore_wait(beyond.at[which], 1)
        tell(rest.at[which], beside(2 - 4 * which))

    state = transform(
        pieces, rim, own_proj, metas, me * ROWS, n_atoms, wq, wo, wu, wd,
        functools.partial(pass_on, near_side),
    )
    atoms = state.astype(bf16)
    means, proj = tokens(atoms, match, counts, wt[...], wp[...])
    mine[0] = proj[0:2, :D]
    mine[1] = proj[0:2, D:]
    slot = lax.rem(wide, 32) * NX + x

    def send_columns(zd, _, part):
        ahead = lax.rem((z - zd) * (1 - 2 * near_side) + NZ, NZ)
        beside_me = (ahead <= 2) | (ahead >= NZ - 2)
        this = (beside_me, (ahead > 2) & (ahead <= 8), (ahead > 8) & (ahead < NZ - 2))[part]

        @pl.when(this)
        def _():
            for dy in (2, 1, 3, 0):
                for dc in (1, 0):
                    to = device(lax.rem(y + dy, NY), zd, lax.rem(core + dc, 2), y)
                    copy = pltpu.make_async_remote_copy(
                        mine.at[1], colbuf.at[slot], csend, crecv, to, MESH
                    )
                    if dy or dc:
                        copy.start()
                    else:
                        pl.when(jnp.logical_not(home & (z == zd)))(copy.start)

        return 0

    def send_part(part):
        lax.fori_loop(0, NZ, functools.partial(send_columns, part=part), 0)

    edge = (z < 4) | (z >= NZ - 4)
    pl.when(edge)(functools.partial(pass_on, 1 - near_side))
    pl.when(z < 4)(functools.partial(send_part, 0))
    pl.semaphore_wait(rest.at[near_side], 1)
    send_part(1)
    pl.when(jnp.logical_not(edge))(functools.partial(pass_on, 1 - near_side))
    pl.when(z >= 4)(functools.partial(send_part, 0))
    pl.semaphore_wait(rest.at[1 - near_side], 1)
    send_part(2)
    pl.when(home)(
        pltpu.make_async_copy(mine.at[1], colbuf.at[slot], crecv).start
    )
    for d in range(1, NX):
        pltpu.make_async_remote_copy(
            mine.at[0], rowbuf.at[x], rsend, rrecv, (wide, lax.rem(x + d, NX)), MESH
        ).start()
    rowbuf[pl.ds(x, 1)] = proj[0:2, :D].reshape(1, 2, D)
    atom_out[...] = atoms[:ROWS]
    single[...] = means[0:2]

    three = rowbuf.at[pl.ds(0, 3)]
    pltpu.make_async_copy(three, three, rrecv).wait()
    for s in range(NX):
        rows_out[pl.ds(2 * s, 2), :] = rowbuf[s].astype(f32)
    pltpu.make_async_copy(colbuf, colbuf, crecv).wait()
    for s in range(128):
        cols_out[pl.ds(2 * s, 2), :] = colbuf[s].astype(f32)
    for s in sends:
        s.wait_send()
    pltpu.make_async_copy(three, three, rsend).wait()
    less = colbuf.at[pl.ds(0, 127)]
    pl.when(home)(pltpu.make_async_copy(less, less, csend).wait)
    pl.when(jnp.logical_not(home))(pltpu.make_async_copy(colbuf, colbuf, csend).wait)


def finish(pair, rows, cols, atoms, means, pair_out, atom_out, single, sums, sem):
    copies = [
        pltpu.make_async_copy(atoms, atom_out, sem.at[0]),
        pltpu.make_async_copy(means, single, sem.at[1]),
    ]
    for copy in copies:
        copy.start()
    cols = cols[...]
    for r in range(8):
        sums[r] = ((pair[r].astype(f32) + rows[pl.ds(r, 1), :]) + cols).astype(bf16)
        copies.append(pltpu.make_async_copy(sums.at[r], pair_out.at[r], sem.at[r + 2]))
        copies[-1].start()
    for copy in copies:
        copy.wait()


def on_device(
    atom_feats, atom_token, key_offset, pair_in, w_qkv, w_out, w_up, w_down, w_tok, w_row, w_col
):
    vmem = pl.BlockSpec(memory_space=pltpu.VMEM)
    hbm = pl.BlockSpec(memory_space=pltpu.HBM)
    dma, flag = pltpu.SemaphoreType.DMA, pltpu.SemaphoreType.REGULAR
    atoms, means, row_vecs, col_vecs = pl.pallas_call(
        functools.partial(kernel, 512 * ROWS),
        out_shape=[
            jax.ShapeDtypeStruct((ROWS, D), bf16),
            jax.ShapeDtypeStruct((2, TOKC), bf16),
            jax.ShapeDtypeStruct((8, D), f32),
            jax.ShapeDtypeStruct((256, D), f32),
        ],
        in_specs=[hbm] * 10,
        out_specs=[vmem] * 4,
        scratch_shapes=[
            pltpu.VMEM((3, ROWS + 16, D), bf16),
            pltpu.VMEM((RIM, D), bf16),
            pltpu.VMEM((1, ROWS), jnp.int32),
            pltpu.VMEM((1, 4), jnp.int32),
            pltpu.VMEM((2, D, 3 * D), bf16),
            pltpu.VMEM((2, D, D), bf16),
            pltpu.VMEM((2, D, 2 * FFH), bf16),
            pltpu.VMEM((2, FFH, D), bf16),
            pltpu.VMEM((D, TOKC), bf16),
            pltpu.VMEM((TOKC, 2 * D), bf16),
            pltpu.VMEM((2, 2, D), bf16),
            pltpu.VMEM((NX, 2, D), bf16),
            pltpu.VMEM((128, 2, D), bf16),
            dma((10,)), dma((3,)), dma((3,)), dma, dma, dma, dma, flag, flag((2,)), flag((2,)),
        ],
        compiler_params=pltpu.CompilerParams(
            collective_id=1, has_side_effects=True, vmem_limit_bytes=32 * 1024 * 1024
        ),
        name="atoms_tokens",
    )(
        *[
            pltpu.with_memory_space_constraint(a, pltpu.HBM)
            for a in (
                atom_feats, atom_token.reshape(1, ROWS), key_offset.reshape(1, 4),
                w_qkv, w_out, w_up, w_down, w_tok, w_row, w_col,
            )
        ]
    )
    pair_out, atom_out, single = pl.pallas_call(
        finish,
        out_shape=[
            jax.ShapeDtypeStruct(pair_in.shape, bf16),
            jax.ShapeDtypeStruct((ROWS, D), bf16),
            jax.ShapeDtypeStruct((2, TOKC), bf16),
        ],
        in_specs=[vmem] * 5,
        out_specs=[hbm] * 3,
        scratch_shapes=[pltpu.VMEM(pair_in.shape, bf16), dma((10,))],
        compiler_params=pltpu.CompilerParams(vmem_limit_bytes=16 * 1024 * 1024),
        name="pair_add",
    )(pair_in, row_vecs, col_vecs, atoms, means)
    return (atom_out, single, pair_out)


def solution(mesh):
    return jax.shard_map(
        on_device,
        mesh=mesh,
        in_specs=(
            P(("wide", "col"), None),
            P(("wide", "col")),
            P(("wide", "col")),
            P("wide", "col", None),
            P(), P(), P(), P(), P(), P(), P(),
        ),
        out_specs=(P(("wide", "col"), None), P(("wide", "col"), None), P("wide", "col", None)),
        check_vma=False,
    )
```
